1024 devices in a mesh: ctx: 16 (over z_hi, y), exp: 64 (over z_lo, x, core).
Axes of the slice: x: 8, y: 8, z: 8 (z_hi: 2, z_lo: 4; z = z_hi * 4 + z_lo), core: 2. Of those that a mesh axis runs over, the one named last changes fastest.
Arguments:
- out_grad: bfloat16 [2048, 8192], P('ctx', 'exp'), may hold values from -6 to 6
- expert_rows: bfloat16 [16, 512, 8192], P('ctx', None, 'exp'), may hold values from -6 to 6
- expert_index: int32 [2048, 2], P('ctx'), may hold values from 0 to 15, all different within a row; in each aligned block of 128 rows (0 to 127, 128 to 255, ...) at most 32 rows name the same one
- combine: float32 [2048, 2], P('ctx'), may hold values from 0.2 to 1
- head_query: bfloat16 [2048, 8192], P('ctx', 'exp'), may hold values from -16 to 16
- head_key: bfloat16 [2048, 1024], P('ctx'), may hold values from -16 to 16
- head_value: bfloat16 [2048, 1024], P('ctx'), may hold values from -6 to 6
- out_weight: bfloat16 [8192, 8192], P('exp'), may hold values from -0.0625 to 0.0625
Outputs:
- residual_grad: bfloat16 [2048, 8192], P('ctx', 'exp')
- query_grad: bfloat16 [2048, 8192], P('ctx', 'exp')
- key_grad: bfloat16 [2048, 1024], P(('ctx', 'exp'))
- value_grad: bfloat16 [2048, 1024], P(('ctx', 'exp'))
The draws below stay inside these ranges and needn't reach their ends.
Inputs may be any that keep to these rules, and one draw needn't show every extreme that they name: `expert_index`: each row names 2 different experts. Among the rows of one index of ctx (aligned blocks of 128 rows) no expert is named by more than 32 rows.
All inputs are finite; a program needn't handle non-finite values.
Results may differ from the reference program's by a relative error of at most 0.02.
Values may be sent and summed in bfloat16 or wider, within the bound.
No kernel may reach another device: no remote copies, remote signals or barrier semaphores. Data moves between devices by JAX's collectives and lax.ppermute only.
A program may use at most 32 MiB of HBM per device.

```python
import math
import jax
import jax.numpy as jnp
import numpy as np
from jax import lax

D = 8192
HEADS = 64
KV_HEADS = 8
HD = 128
TOP = 2
TOK_CTX = 128
EXPERTS = 16
TOKENS = 2048
GROUP = 8
KV_D = 1024
CAP = 32
SLOTS = 512
N_CTX = 16


def draw_head_query(key, part):
    key = jax.random.fold_in(key, 1)
    return jnp.clip(jax.random.normal(key, (TOKENS, D), jnp.float32), -6.0, 6.0).astype(jnp.bfloat16)


def draw_head_key(key, part):
    key = jax.random.fold_in(key, 2)
    return jnp.clip(jax.random.normal(key, (TOKENS, KV_D), jnp.float32), -6.0, 6.0).astype(jnp.bfloat16)


def shard_levels(rng, extent, shards, least, top_value):
    gain = 1.0
    for axis_at, shards_of in shards:
        heights = jax.random.uniform(jax.random.fold_in(jax.random.fold_in(rng, 6), axis_at), (shards_of,), jnp.float32, least / len(shards), top_value / len(shards))
        gain = gain * jnp.repeat(jnp.exp(heights), extent[axis_at] // shards_of).reshape((-1,) + (1,) * (len(extent) - 1 - axis_at))
    return gain


def deal_out(stream_key, own, number, rows, number_of, top, reach, lean):
    sequence = jax.random.permutation(stream_key, number_of)
    packed, usual = load_shares(number_of, rows * top, reach, lean, True), load_shares(number_of, rows * top, reach, lean, False)
    places = jnp.arange(number_of)

    def named(tallies, turn):
        used = int((tallies > 0).sum())
        fixed = max(1, used // 4)
        passed = fixed + (places - fixed + turn * (used - fixed)) % max(1, number_of - fixed)
        return jnp.zeros((number_of,), jnp.int32).at[sequence[jnp.where(places < fixed, places, passed)]].set(jnp.asarray(tallies, jnp.int32))

    tallies = jnp.where(number % 4 == 0, named(packed, number // 4), named(usual, number - number // 4 - 1))
    mixed = jax.random.permutation(jax.random.fold_in(own, 3), number_of)
    source_of, sink = mixed[0:number_of // 2 * 2:2], mixed[1:number_of // 2 * 2:2]
    room = jnp.minimum(tallies[source_of] - 1, reach - tallies[sink]) // 2
    room = jnp.where((source_of == sequence[0]) | (sink == sequence[0]) | (tallies[sink] == 0), 0, jnp.maximum(room, 0))
    passed = jax.random.randint(jax.random.fold_in(own, 4), (number_of // 2,), 0, 1 << 20) % (room + 1)
    tallies = tallies.at[source_of].add(-passed).at[sink].add(passed)
    items = jnp.searchsorted(jnp.cumsum(tallies), jnp.arange(rows * top), side="right").astype(jnp.int32)
    table = items.reshape(top, rows).T
    table = table[jax.random.permutation(jax.random.fold_in(own, 1), rows)]
    turn = jax.random.randint(jax.random.fold_in(own, 2), (rows, 1), 0, top)
    return jnp.take_along_axis(table, (jnp.arange(top)[None, :] + turn) % top, axis=1)


def load_shares(number_of, total, most, skew, full):
    portions = [(1 << 20) // math.isqrt(grade ** skew) + 1 for grade in range(1, number_of + 1)]
    largest = most if full else min(most, max(-(-total // number_of), total * portions[0] // sum(portions)))
    least = 1 if total - largest >= number_of - 1 else 0
    holding, spare = [largest] + [least] * (number_of - 1), total - largest - least * (number_of - 1)
    while spare > 0:
        movable = [i for i in range(1, number_of) if holding[i] < largest] or [i for i in range(1, number_of) if holding[i] < most]
        mass, left = sum([portions[i] for i in movable]), spare
        for i in movable:
            addition = min(most - holding[i], max(1, left * portions[i] // mass), spare)
            holding[i] = holding[i] + addition
            spare = spare - addition
    return np.array(holding)


def scatter_about(own_key, extent, scale, reach, cuts=(), kind=jnp.bfloat16):
    gain = shard_levels(own_key, extent, cuts, -0.22, 0.18) if cuts else 1.0
    values = jax.random.normal(own_key, extent, jnp.float32) * scale * gain
    return jnp.minimum(jnp.maximum(values, -reach), reach).astype(kind)


def setup_inputs(seed: int = 0) -> dict:
    streams_of = jax.random.split(jax.random.key(seed), 9)
    out_grad = scatter_about(streams_of[0], (TOKENS, D), 1.0, 6.0, ((0, 16), (1, 64)))
    expert_rows = scatter_about(streams_of[1], (EXPERTS, SLOTS, D), 1.0, 6.0, ((0, 16), (2, 64)))
    expert_index_keys = jax.random.split(jax.random.fold_in(streams_of[2], 1), TOKENS // TOK_CTX)
    expert_index_turns = jax.random.permutation(jax.random.fold_in(streams_of[2], 3), TOKENS // TOK_CTX)
    expert_index = jax.vmap(lambda own, number: deal_out(jax.random.fold_in(streams_of[2], 2), own, number, TOK_CTX, EXPERTS, TOP, CAP, 2))(expert_index_keys, expert_index_turns).reshape((TOKENS, TOP))
    combine = jnp.clip(0.2 + 0.8 * jax.random.uniform(streams_of[3], (TOKENS, TOP), jnp.float32) ** shard_levels(streams_of[3], (TOKENS, TOP), ((0, 16),), -0.2, 0.2), 0.2, 1.0)
    head_query = draw_head_query(jax.random.fold_in(streams_of[8], 71), 0)
    head_key = draw_head_key(jax.random.fold_in(streams_of[8], 71), 0)
    head_value = scatter_about(streams_of[6], (TOKENS, KV_D), 1.0, 6.0, ((0, 16),))
    out_weight = scatter_about(streams_of[7], (D, D), D ** -0.5, 0.0625, ((0, 64),))
    return dict(out_grad=out_grad, expert_rows=expert_rows, expert_index=expert_index, combine=combine, head_query=head_query, head_key=head_key, head_value=head_value, out_weight=out_weight)


def folded_positions(row_ids, per_device, ctx_count):
    half_rows = per_device // 2
    device = row_ids // per_device
    within = row_ids % per_device
    block = jnp.where(within < half_rows, device, 2 * ctx_count - 1 - device)
    return (block * half_rows + within % half_rows).astype(jnp.int32)


def to_heads(array, count):
    return jnp.transpose(array.reshape(TOKENS, count, HD), (1, 0, 2))


def from_heads(array, count):
    return jnp.transpose(array, (1, 0, 2)).reshape(TOKENS, count * HD)


def reference(out_grad, expert_rows, expert_index, combine, head_query, head_key, head_value, out_weight):
    flat = expert_index.reshape(N_CTX, TOK_CTX * TOP)
    onehot = (flat[:, :, None] == jnp.arange(EXPERTS, dtype=jnp.int32)[None, None, :]).astype(jnp.int32)
    earlier = jnp.cumsum(onehot, axis=1) - onehot
    slot_ids = jnp.sum(earlier * onehot, axis=2).reshape(TOKENS, TOP).astype(jnp.int32)
    source = (jnp.arange(TOKENS, dtype=jnp.int32) // TOK_CTX)[:, None]
    picked = expert_rows[expert_index, source * CAP + slot_ids]
    moe_grad = jnp.sum(combine[:, :, None] * picked.astype(jnp.float32), axis=1)
    residual_grad = (out_grad.astype(jnp.float32) + moe_grad).astype(jnp.bfloat16)
    context_grad = jnp.dot(residual_grad, out_weight.T, preferred_element_type=jnp.float32).astype(jnp.bfloat16)
    position = folded_positions(jnp.arange(TOKENS, dtype=jnp.int32), TOK_CTX, N_CTX)
    allowed = position[None, :] <= position[:, None]
    score_scale = 1.0 / (HD ** 0.5)

    def one_head(operands):
        query_one, key_one, value_one, grad_one = operands
        scores = jnp.dot(query_one, key_one.T, preferred_element_type=jnp.float32) * score_scale
        masked = jnp.where(allowed, scores, -jnp.inf)
        row_max = jnp.max(masked, axis=1, keepdims=True)
        exponent = jnp.where(allowed, jnp.exp(masked - row_max), 0.0)
        probs = exponent / jnp.sum(exponent, axis=1, keepdims=True)
        probs_low = probs.astype(jnp.bfloat16)
        head_out = jnp.dot(probs_low, value_one, preferred_element_type=jnp.float32)
        row_delta = jnp.sum(grad_one.astype(jnp.float32) * head_out, axis=1, keepdims=True)
        prob_grad = jnp.dot(grad_one, value_one.T, preferred_element_type=jnp.float32)
        score_grad = probs * (prob_grad - row_delta)
        score_low = score_grad.astype(jnp.bfloat16)
        query_part = jnp.dot(score_low, key_one, preferred_element_type=jnp.float32) * score_scale
        key_part = jnp.dot(score_low.T, query_one, preferred_element_type=jnp.float32) * score_scale
        value_part = jnp.dot(probs_low.T, grad_one, preferred_element_type=jnp.float32)
        return (query_part.astype(jnp.bfloat16), key_part, value_part)

    key_rep = jnp.repeat(to_heads(head_key, KV_HEADS), GROUP, axis=0)
    value_rep = jnp.repeat(to_heads(head_value, KV_HEADS), GROUP, axis=0)
    query_all, key_all, value_all = lax.map(one_head, (to_heads(head_query, HEADS), key_rep, value_rep, to_heads(context_grad, HEADS)))
    key_sum = jnp.sum(key_all.reshape(KV_HEADS, GROUP, TOKENS, HD), axis=1).astype(jnp.bfloat16)
    value_sum = jnp.sum(value_all.reshape(KV_HEADS, GROUP, TOKENS, HD), axis=1).astype(jnp.bfloat16)
    return (residual_grad, from_heads(query_all, HEADS), from_heads(key_sum, KV_HEADS), from_heads(value_sum, KV_HEADS))
```

```python
import math

import jax
import jax.numpy as jnp
from jax import lax
from jax.experimental import pallas as pl
from jax.experimental.pallas import tpu as pltpu
from jax.sharding import Mesh
from jax.sharding import PartitionSpec as P

HD = 128
SCALE = 1.0 / math.sqrt(HD)
LOW = -1e30
AXES = ("zh", "y", "zl", "xh", "xl", "core")
SIZES = (2, 8, 4, 2, 4, 2)
CTX = ("zh", "y")
EXP = ("zl", "xh", "xl", "core")
PEERS = ("zl", "xh", "xl")
N_CTX = 16
ROWS = 128
EXPERTS = 16
CAP = 32
N_PEERS = 32
HALF = 64
KEYS = N_CTX * HALF
F32 = jnp.float32
BF16 = jnp.bfloat16
VMEM = pl.BlockSpec(memory_space=pltpu.VMEM)
PARAMS = pltpu.CompilerParams(vmem_limit_bytes=40 * 1024 * 1024)


def call(kernel, outs, *operands):
    return pl.pallas_call(
        kernel,
        out_shape=[jax.ShapeDtypeStruct(shape, kind) for shape, kind in outs],
        in_specs=[VMEM] * len(operands),
        out_specs=[VMEM] * len(outs),
        compiler_params=PARAMS,
    )(*operands)


def dot(a, b, dims):
    return lax.dot_general(a, b, ((dims[:1], dims[1:]), ((), ())), preferred_element_type=F32)


def iota(shape, dim):
    return lax.broadcasted_iota(jnp.int32, shape, dim)


def key_row(number):
    xl, zl, xh, i = number // 16, (number // 4) % 4, (number // 2) % 2, number % 2
    return zl * 32 + xh * 16 + xl * 4 + lax.axis_index("core") * 2 + i


def position(block, row):
    return jnp.where(row < 64, block, 2 * N_CTX - 1 - block) * 64 + row % 64


def keys_kernel(key_ref, value_ref, out_ref):
    group = lax.axis_index("zl") * 2 + lax.axis_index("xh")
    columns = pl.ds(pl.multiple_of(group * HD, HD), HD)
    select = (iota((HALF, ROWS), 1) == key_row(iota((HALF, ROWS), 0))).astype(BF16)
    chosen = jnp.concatenate(
        [
            dot(select, key_ref[:, columns], (1, 0)),
            dot(select, value_ref[:, columns], (1, 0)),
        ],
        axis=1,
    ).astype(BF16)
    for c in range(N_CTX):
        out_ref[c] = chosen


def weight_kernel(weight_ref, query_ref, own_ref, send_ref):
    core = lax.axis_index("core")
    for b in range(N_PEERS):
        there = slice(b * HD, (b + 1) * HD)
        own_ref[:, there] = weight_ref[:, pl.ds(pl.multiple_of((2 * b + core) * HD, HD), HD)]
        send_ref[:, there] = weight_ref[:, pl.ds(pl.multiple_of((2 * b + 1 - core) * HD, HD), HD)]
    send_ref[:, N_PEERS * HD :] = query_ref[...]


def slots_kernel(index_ref, out_ref):
    index = index_ref[...]
    experts = iota((ROWS, HD), 1)
    named = [index[:, k : k + 1] == experts for k in range(2)]
    both = (named[0] | named[1]).astype(BF16)
    before = (iota((ROWS, ROWS), 1) < iota((ROWS, ROWS), 0)).astype(BF16)
    earlier = dot(before, both, (1, 0))
    for k in range(2):
        slot = jnp.sum(jnp.where(named[k], earlier, 0.0), axis=1, keepdims=True).astype(jnp.int32)
        place = index[:, k : k + 1] * CAP + slot
        wide = iota((ROWS, EXPERTS * CAP), 1) == place
        out_ref[k * ROWS : (k + 1) * ROWS] = wide.astype(BF16)


def residual_kernel(grad_ref, rows_ref, onehot_ref, combine_ref, out_ref, send_ref):
    rows = rows_ref[...].reshape(EXPERTS * CAP, HD)
    picked = dot(onehot_ref[...], rows, (1, 0))
    combine = combine_ref[...]
    moe = combine[:, 0:1] * picked[:ROWS] + combine[:, 1:2] * picked[ROWS:]
    residual = (grad_ref[...].astype(F32) + moe).astype(BF16)
    out_ref[...] = residual
    for b in range(N_PEERS):
        send_ref[b] = residual


def forward_kernel(query_ref, mate_ref, kv_ref, probs_ref, stat_ref):
    block = lax.axis_index("zh") * 8 + lax.axis_index("y")
    query = jnp.concatenate([query_ref[...], mate_ref[:, N_PEERS * HD :]], axis=0)
    kv = kv_ref[...].reshape(KEYS, 2 * HD)
    row = iota((2 * ROWS, 1), 0) % ROWS
    number = iota((1, KEYS), 1)
    allowed = position(number // HALF, key_row(number % HALF)) <= position(block, row)
    scores = jnp.where(allowed, dot(query, kv[:, :HD], (1, 1)) * SCALE, LOW)
    top = jnp.max(scores, axis=1, keepdims=True)
    probs = jnp.where(allowed, jnp.exp(scores - top), 0.0)
    total = jnp.sum(probs, axis=1, keepdims=True)
    probs_ref[...] = probs
    stat_ref[:, :HD] = dot(probs.astype(BF16), kv[:, HD:], (1, 0))
    stat_ref[:, HD:] = jnp.where(iota((2 * ROWS, HD), 1) < HALF, top, total)


def project_kernel(blocks_ref, own_ref, mate_ref, out_ref):
    total = [jnp.zeros((ROWS, HD), F32)] * 2
    for a in range(0, N_PEERS, 8):
        part = jnp.concatenate([blocks_ref[b] for b in range(a, a + 8)], axis=1)
        there = slice(a * HD, (a + 8) * HD)
        total = [
            total[0] + dot(part, own_ref[:, there], (1, 1)),
            total[1] + dot(part, mate_ref[:, there], (1, 1)),
        ]
    out_ref[:, :HD] = total[0]
    out_ref[:, HD:] = total[1]


def backward_kernel(
    part_ref, other_ref, query_ref, mate_ref, kv_ref, probs_ref, stat_ref, seen_ref,
    kv_grad_ref, own_ref, send_ref,
):
    grad = jnp.concatenate(
        [
            part_ref[:, :HD] + other_ref[:, HD:],
            part_ref[:, HD:] + other_ref[:, :HD],
        ],
        axis=0,
    ).astype(BF16)
    query = jnp.concatenate([query_ref[...], mate_ref[:, N_PEERS * HD :]], axis=0)
    kv = kv_ref[...].reshape(KEYS, 2 * HD)
    mine = stat_ref[...]
    seen = jnp.concatenate([seen_ref[ROWS:], seen_ref[:ROWS]], axis=0)
    top_mine, top_seen = mine[:, HD : HD + 1], seen[:, HD : HD + 1]
    top = jnp.maximum(top_mine, top_seen)
    mine_gain, seen_gain = jnp.exp(top_mine - top), jnp.exp(top_seen - top)
    total = mine[:, HD + HALF : HD + HALF + 1] * mine_gain + seen[:, HD + HALF : HD + HALF + 1] * seen_gain
    mine_gain, seen_gain = mine_gain / total, seen_gain / total
    head_out = mine[:, :HD] * mine_gain + seen[:, :HD] * seen_gain
    delta = jnp.sum(grad.astype(F32) * head_out, axis=1, keepdims=True)
    probs = probs_ref[...] * mine_gain
    score_grad = (probs * (dot(grad, kv[:, HD:], (1, 1)) - delta)).astype(BF16)
    kv_grad_ref[:, :, :HD] = (dot(score_grad, query, (0, 0)) * SCALE).astype(BF16).reshape(HALF, 16, HD)
    kv_grad_ref[:, :, HD:] = dot(probs.astype(BF16), grad, (0, 0)).astype(BF16).reshape(HALF, 16, HD)
    query_grad = dot(score_grad, kv[:, :HD], (1, 0)) * SCALE
    own_ref[...] = query_grad[:ROWS]
    send_ref[...] = query_grad[ROWS:]


def sum_kernel(parts_ref, out_ref):
    out_ref[...] = jnp.sum(parts_ref[...].astype(F32), axis=0).astype(BF16)


def swap(array):
    return lax.ppermute(array, "core", [(0, 1), (1, 0)])


def body(out_grad, expert_rows, expert_index, combine, head_query, head_key, head_value, out_weight):
    received = lax.all_to_all(
        expert_rows.reshape(N_CTX, CAP, HD), CTX, split_axis=0, concat_axis=0, tiled=True
    )
    (kv_send,) = call(keys_kernel, [((N_CTX, HALF, 2 * HD), BF16)], head_key, head_value)
    kv_all = lax.all_to_all(kv_send, CTX, split_axis=0, concat_axis=0, tiled=True)
    own_weight, send_weight = call(
        weight_kernel,
        [((ROWS, N_PEERS * HD), BF16), ((ROWS, (N_PEERS + 1) * HD), BF16)],
        out_weight,
        head_query,
    )
    mate = swap(send_weight)
    (onehot,) = call(slots_kernel, [((2 * ROWS, EXPERTS * CAP), BF16)], expert_index)
    residual_grad, residual_send = call(
        residual_kernel,
        [((ROWS, HD), BF16), ((N_PEERS, ROWS, HD), BF16)],
        out_grad,
        received,
        onehot,
        combine,
    )
    blocks = lax.all_to_all(residual_send, PEERS, split_axis=0, concat_axis=0, tiled=True)
    probs, stat = call(
        forward_kernel,
        [((2 * ROWS, KEYS), F32), ((2 * ROWS, 2 * HD), F32)],
        head_query,
        mate,
        kv_all,
    )
    seen = swap(stat)
    (part,) = call(project_kernel, [((ROWS, 2 * HD), F32)], blocks, own_weight, mate)
    other = swap(part)
    kv_grad, own_grad, send_grad = call(
        backward_kernel,
        [((HALF, 16, 2 * HD), BF16), ((ROWS, HD), F32), ((ROWS, HD), F32)],
        part,
        other,
        head_query,
        mate,
        kv_all,
        probs,
        stat,
        seen,
    )
    kv_parts = lax.all_to_all(kv_grad, ("zh", "y", "xl"), split_axis=0, concat_axis=0, tiled=True)
    query_grad = (own_grad + swap(send_grad)).astype(BF16)
    (kv_sum,) = call(sum_kernel, [((16, 2 * HD), BF16)], kv_parts)
    final = lax.all_to_all(
        kv_sum.reshape(8, 2, 2 * HD), ("zl", "xh"), split_axis=0, concat_axis=0, tiled=True
    )
    final = jnp.transpose(final, (1, 0, 2))
    key_grad = final[:, :, :HD].reshape(2, 8 * HD)
    value_grad = final[:, :, HD:].reshape(2, 8 * HD)
    return residual_grad, query_grad, key_grad, value_grad


def solution(mesh):
    fine = Mesh(mesh.devices.reshape(SIZES), AXES)
    in_specs = (
        P(CTX, EXP),
        P(CTX, None, EXP),
        P(CTX, None),
        P(CTX, None),
        P(CTX, EXP),
        P(CTX, None),
        P(CTX, None),
        P(EXP, None),
    )
    out_specs = (P(CTX, EXP), P(CTX, EXP), P(CTX + EXP, None), P(CTX + EXP, None))
    return jax.shard_map(body, mesh=fine, in_specs=in_specs, out_specs=out_specs, check_vma=False)
```

```python
import math

import jax
import jax.numpy as jnp
from jax import lax
from jax.experimental import pallas as pl
from jax.experimental.pallas import tpu as pltpu
from jax.sharding import Mesh
from jax.sharding import PartitionSpec as P

HD = 128
SCALE = 1.0 / math.sqrt(HD)
LOW = -1e30
AXES = ("zh", "y", "zl", "xh", "xl", "core")
SIZES = (2, 8, 4, 2, 4, 2)
CTX = ("zh", "y")
EXP = ("zl", "xh", "xl", "core")
PEERS = ("zl", "xh", "xl")
N_CTX = 16
ROWS = 128
EXPERTS = 16
CAP = 32
N_PEERS = 32
HALF = 64
KEYS = N_CTX * HALF
PACK = CAP + 2 * HALF
F32 = jnp.float32
BF16 = jnp.bfloat16
VMEM = pl.BlockSpec(memory_space=pltpu.VMEM)
PARAMS = pltpu.CompilerParams(vmem_limit_bytes=16 * 1024 * 1024)


def call(kernel, outs, *operands):
    return pl.pallas_call(
        kernel,
        out_shape=[jax.ShapeDtypeStruct(shape, kind) for shape, kind in outs],
        in_specs=[VMEM] * len(operands),
        out_specs=[VMEM] * len(outs),
        compiler_params=PARAMS,
    )(*operands)


def dot(a, b, dims):
    return lax.dot_general(a, b, ((dims[:1], dims[1:]), ((), ())), preferred_element_type=F32)


def iota(shape, dim):
    return lax.broadcasted_iota(jnp.int32, shape, dim)


def key_row(number):
    xl, zl, xh, i = number // 16, (number // 4) % 4, (number // 2) % 2, number % 2
    return zl * 32 + xh * 16 + xl * 4 + lax.axis_index("core") * 2 + i


def position(block, row):
    return jnp.where(row < 64, block, 2 * N_CTX - 1 - block) * 64 + row % 64


def received_kv(pack_ref):
    return (
        pack_ref[:, CAP : CAP + HALF].reshape(KEYS, HD),
        pack_ref[:, CAP + HALF :].reshape(KEYS, HD),
    )


def pack_kernel(rows_ref, key_ref, value_ref, out_ref, key_own, value_own, sems):
    group = lax.axis_index("zl") * 2 + lax.axis_index("xh")
    columns = pl.ds(pl.multiple_of(group * HD, HD), HD)
    copies = [
        pltpu.make_async_copy(key_ref.at[:, columns], key_own, sems.at[0]),
        pltpu.make_async_copy(value_ref.at[:, columns], value_own, sems.at[1]),
    ]
    for copy in copies:
        copy.start()
    out_ref[:, :CAP] = rows_ref[...]
    select = (iota((HALF, ROWS), 1) == key_row(iota((HALF, ROWS), 0))).astype(BF16)
    for copy in copies:
        copy.wait()
    keys = dot(select, key_own[...], (1, 0)).astype(BF16)
    values = dot(select, value_own[...], (1, 0)).astype(BF16)
    for c in range(N_CTX):
        out_ref[c, CAP : CAP + HALF] = keys
        out_ref[c, CAP + HALF :] = values


def weight_kernel(weight_ref, query_ref, own_ref, send_ref):
    core = lax.axis_index("core")
    for b in range(N_PEERS):
        there = slice(b * HD, (b + 1) * HD)
        own_ref[:, there] = weight_ref[:, pl.ds(pl.multiple_of((2 * b + core) * HD, HD), HD)]
        send_ref[:, there] = weight_ref[:, pl.ds(pl.multiple_of((2 * b + 1 - core) * HD, HD), HD)]
    send_ref[:, N_PEERS * HD :] = query_ref[...]


def slots_kernel(index_ref, out_ref):
    index = index_ref[...]
    experts = iota((ROWS, HD), 1)
    named = [index[:, k : k + 1] == experts for k in range(2)]
    both = (named[0] | named[1]).astype(BF16)
    before = (iota((ROWS, ROWS), 1) < iota((ROWS, ROWS), 0)).astype(BF16)
    earlier = dot(before, both, (1, 0))
    for k in range(2):
        slot = jnp.sum(jnp.where(named[k], earlier, 0.0), axis=1, keepdims=True).astype(jnp.int32)
        place = index[:, k : k + 1] * CAP + slot
        wide = iota((ROWS, EXPERTS * CAP), 1) == place
        out_ref[k * ROWS : (k + 1) * ROWS] = wide.astype(BF16)


def residual_kernel(grad_ref, pack_ref, onehot_ref, combine_ref, out_ref, send_ref):
    rows = pack_ref[:, :CAP].reshape(EXPERTS * CAP, HD)
    picked = dot(onehot_ref[...], rows, (1, 0))
    combine = combine_ref[...]
    moe = combine[:, 0:1] * picked[:ROWS] + combine[:, 1:2] * picked[ROWS:]
    residual = (grad_ref[...].astype(F32) + moe).astype(BF16)
    out_ref[...] = residual
    for b in range(N_PEERS):
        send_ref[b] = residual


def forward_kernel(query_ref, mate_ref, pack_ref, probs_ref, stat_ref):
    block = lax.axis_index("zh") * 8 + lax.axis_index("y")
    query = jnp.concatenate([query_ref[...], mate_ref[:, N_PEERS * HD :]], axis=0)
    keys, values = received_kv(pack_ref)
    row = iota((2 * ROWS, 1), 0) % ROWS
    number = iota((1, KEYS), 1)
    allowed = position(number // HALF, key_row(number % HALF)) <= position(block, row)
    scores = jnp.where(allowed, dot(query, keys, (1, 1)) * SCALE, LOW)
    top = jnp.max(scores, axis=1, keepdims=True)
    probs = jnp.where(allowed, jnp.exp(scores - top), 0.0)
    total = jnp.sum(probs, axis=1, keepdims=True)
    probs_ref[...] = probs
    stat_ref[:, :HD] = dot(probs.astype(BF16), values, (1, 0))
    stat_ref[:, HD:] = jnp.where(iota((2 * ROWS, HD), 1) < HALF, top, total)


def project_kernel(blocks_ref, own_ref, mate_ref, out_ref):
    total = [jnp.zeros((ROWS, HD), F32)] * 2
    for a in range(0, N_PEERS, 8):
        part = jnp.concatenate([blocks_ref[b] for b in range(a, a + 8)], axis=1)
        there = slice(a * HD, (a + 8) * HD)
        total = [
            total[0] + dot(part, own_ref[:, there], (1, 1)),
            total[1] + dot(part, mate_ref[:, there], (1, 1)),
        ]
    out_ref[:, :HD] = total[0]
    out_ref[:, HD:] = total[1]


def backward_kernel(
    part_ref, other_ref, query_ref, mate_ref, pack_ref, probs_ref, stat_ref, seen_ref,
    kv_grad_ref, own_ref, send_ref,
):
    grad = jnp.concatenate(
        [
            part_ref[:, :HD] + other_ref[:, HD:],
            part_ref[:, HD:] + other_ref[:, :HD],
        ],
        axis=0,
    ).astype(BF16)
    query = jnp.concatenate([query_ref[...], mate_ref[:, N_PEERS * HD :]], axis=0)
    keys, values = received_kv(pack_ref)
    mine = stat_ref[...]
    seen = jnp.concatenate([seen_ref[ROWS:], seen_ref[:ROWS]], axis=0)
    top_mine, top_seen = mine[:, HD : HD + 1], seen[:, HD : HD + 1]
    top = jnp.maximum(top_mine, top_seen)
    mine_gain, seen_gain = jnp.exp(top_mine - top), jnp.exp(top_seen - top)
    total = mine[:, HD + HALF : HD + HALF + 1] * mine_gain + seen[:, HD + HALF : HD + HALF + 1] * seen_gain
    mine_gain, seen_gain = mine_gain / total, seen_gain / total
    head_out = mine[:, :HD] * mine_gain + seen[:, :HD] * seen_gain
    delta = jnp.sum(grad.astype(F32) * head_out, axis=1, keepdims=True)
    probs = probs_ref[...] * mine_gain
    score_grad = (probs * (dot(grad, values, (1, 1)) - delta)).astype(BF16)
    key_grad = (dot(score_grad, query, (0, 0)) * SCALE).astype(BF16).reshape(2, 32, 16, HD)
    value_grad = dot(probs.astype(BF16), grad, (0, 0)).astype(BF16).reshape(2, 32, 16, HD)
    for zh in range(2):
        kv_grad_ref[:, zh * 16 : (zh + 1) * 16, :HD] = key_grad[zh]
        kv_grad_ref[:, zh * 16 : (zh + 1) * 16, HD:] = value_grad[zh]
    query_grad = dot(score_grad, keys, (1, 0)) * SCALE
    own_ref[...] = query_grad[:ROWS]
    send_ref[...] = query_grad[ROWS:]


def sum_kernel(parts_ref, out_ref):
    total = parts_ref[0].astype(F32)
    for b in range(1, 32):
        total = total + parts_ref[b].astype(F32)
    low = total.astype(BF16)
    row, source = iota((64, 32), 0), iota((64, 32), 1)
    place = row // 4 * 2 + row % 2
    pick_key = ((place == source) & (row // 2 % 2 == 0)).astype(BF16)
    pick_value = ((place == source) & (row // 2 % 2 == 1)).astype(BF16)
    out_ref[...] = (dot(pick_key, low[:, :HD], (1, 0)) + dot(pick_value, low[:, HD:], (1, 0))).astype(BF16)


def last_kernel(parts_ref, key_ref, value_ref):
    parts = parts_ref[...].astype(F32)
    total = parts[:32] + parts[32:]
    key_ref[...] = jnp.concatenate([total[4 * g : 4 * g + 2] for g in range(8)], axis=1).astype(BF16)
    value_ref[...] = jnp.concatenate([total[4 * g + 2 : 4 * g + 4] for g in range(8)], axis=1).astype(BF16)


def swap(array):
    return lax.ppermute(array, "core", [(0, 1), (1, 0)])


def exchange(array, axes):
    return lax.all_to_all(array, axes, split_axis=0, concat_axis=0, tiled=True)


def body(out_grad, expert_rows, expert_index, combine, head_query, head_key, head_value, out_weight):
    packed = pl.pallas_call(
        pack_kernel,
        out_shape=jax.ShapeDtypeStruct((N_CTX, PACK, HD), BF16),
        in_specs=[VMEM, pl.BlockSpec(memory_space=pl.ANY), pl.BlockSpec(memory_space=pl.ANY)],
        out_specs=VMEM,
        scratch_shapes=[
            pltpu.VMEM((ROWS, HD), BF16),
            pltpu.VMEM((ROWS, HD), BF16),
            pltpu.SemaphoreType.DMA((2,)),
        ],
        compiler_params=PARAMS,
    )(expert_rows.reshape(N_CTX, CAP, HD), head_key, head_value)
    received = exchange(packed, CTX)
    own_weight, send_weight = call(
        weight_kernel,
        [((ROWS, N_PEERS * HD), BF16), ((ROWS, (N_PEERS + 1) * HD), BF16)],
        out_weight,
        head_query,
    )
    mate = swap(send_weight)
    (onehot,) = call(slots_kernel, [((2 * ROWS, EXPERTS * CAP), BF16)], expert_index)
    residual_grad, residual_send = call(
        residual_kernel,
        [((ROWS, HD), BF16), ((N_PEERS, ROWS, HD), BF16)],
        out_grad,
        received,
        onehot,
        combine,
    )
    blocks = exchange(residual_send, PEERS)
    probs, stat = call(
        forward_kernel,
        [((2 * ROWS, KEYS), F32), ((2 * ROWS, 2 * HD), F32)],
        head_query,
        mate,
        received,
    )
    seen = swap(stat)
    (part,) = call(project_kernel, [((ROWS, 2 * HD), F32)], blocks, own_weight, mate)
    other = swap(part)
    kv_grad, own_grad, send_grad = call(
        backward_kernel,
        [((32, 32, 2 * HD), BF16), ((ROWS, HD), F32), ((ROWS, HD), F32)],
        part,
        other,
        head_query,
        mate,
        received,
        probs,
        stat,
        seen,
    )
    kv_parts = exchange(kv_grad, ("y", "xl"))
    query_grad = (own_grad + swap(send_grad)).astype(BF16)
    (kv_sum,) = call(sum_kernel, [((64, HD), BF16)], kv_parts)
    final = exchange(kv_sum.reshape(16, 4, HD), ("zh", "zl", "xh"))
    key_grad, value_grad = call(
        last_kernel, [((2, 8 * HD), BF16), ((2, 8 * HD), BF16)], final.reshape(64, HD)
    )
    return residual_grad, query_grad, key_grad, value_grad


def solution(mesh):
    fine = Mesh(mesh.devices.reshape(SIZES), AXES)
    in_specs = (
        P(CTX, EXP),
        P(CTX, None, EXP),
        P(CTX, None),
        P(CTX, None),
        P(CTX, EXP),
        P(CTX, None),
        P(CTX, None),
        P(EXP, None),
    )
    out_specs = (P(CTX, EXP), P(CTX, EXP), P(CTX + EXP, None), P(CTX + EXP, None))
    return jax.shard_map(body, mesh=fine, in_specs=in_specs, out_specs=out_specs, check_vma=False)
```

```python
import math

import jax
import jax.numpy as jnp
from jax import lax
from jax.experimental import pallas as pl
from jax.experimental.pallas import tpu as pltpu
from jax.sharding import Mesh
from jax.sharding import PartitionSpec as P

HD = 128
SCALE = 1.0 / math.sqrt(HD)
LOW = -1e30
AXES = ("zh", "y", "zl", "xh", "xl", "core")
SIZES = (2, 8, 4, 2, 4, 2)
CTX = ("zh", "y")
EXP = ("zl", "xh", "xl", "core")
PEERS = ("zl", "xh", "xl")
N_CTX = 16
ROWS = 128
EXPERTS = 16
CAP = 32
N_PEERS = 32
HALF = 64
KEYS = N_CTX * HALF
QUARTER = 32
PACK = CAP + 2 * QUARTER
F32 = jnp.float32
BF16 = jnp.bfloat16
VMEM = pl.BlockSpec(memory_space=pltpu.VMEM)
HBM = pl.BlockSpec(memory_space=pltpu.HBM)
PARAMS = pltpu.CompilerParams(vmem_limit_bytes=16 * 1024 * 1024)


def call(kernel, outs, *operands):
    return pl.pallas_call(
        kernel,
        out_shape=[jax.ShapeDtypeStruct(shape, kind) for shape, kind in outs],
        in_specs=[VMEM] * len(operands),
        out_specs=[VMEM] * len(outs),
        compiler_params=PARAMS,
    )(*operands)


def dot(a, b, dims):
    return lax.dot_general(a, b, ((dims[:1], dims[1:]), ((), ())), preferred_element_type=F32)


def iota(shape, dim):
    return lax.broadcasted_iota(jnp.int32, shape, dim)


def key_row(number):
    xl, zl, xh, i = number // 16, (number // 4) % 4, (number // 2) % 2, number % 2
    return zl * 32 + xh * 16 + xl * 4 + lax.axis_index("core") * 2 + i


def position(block, row):
    return jnp.where(row < 64, block, 2 * N_CTX - 1 - block) * 64 + row % 64


def half_of(part):
    mine = lax.axis_index("xl") % 2
    return part + mine - 2 * part * mine


def joined_kv(pack_ref, seen_ref):
    return [
        jnp.concatenate(
            [
                pack_ref[:, CAP + at : CAP + at + QUARTER].reshape(KEYS // 2, HD),
                seen_ref[:, at : at + QUARTER].reshape(KEYS // 2, HD),
            ],
            axis=0,
        )
        for at in (0, QUARTER)
    ]


def pack_kernel(rows_ref, key_ref, value_ref, out_ref, key_own, value_own, sems):
    group = lax.axis_index("zl") * 2 + lax.axis_index("xh")
    columns = pl.ds(pl.multiple_of(group * HD, HD), HD)
    copies = [
        pltpu.make_async_copy(key_ref.at[:, columns], key_own, sems.at[0]),
        pltpu.make_async_copy(value_ref.at[:, columns], value_own, sems.at[1]),
        pltpu.make_async_copy(rows_ref, out_ref.at[:, :CAP], sems.at[2]),
    ]
    for copy in copies:
        copy.start()
    number = half_of(0) * QUARTER + iota((QUARTER, ROWS), 0)
    select = (iota((QUARTER, ROWS), 1) == key_row(number)).astype(BF16)
    copies[0].wait()
    copies[1].wait()
    keys = dot(select, key_own[...], (1, 0)).astype(BF16)
    values = dot(select, value_own[...], (1, 0)).astype(BF16)
    for c in range(N_CTX):
        out_ref[c, CAP : CAP + QUARTER] = keys
        out_ref[c, CAP + QUARTER :] = values
    copies[2].wait()


def weight_kernel(weight_ref, send_ref):
    core = lax.axis_index("core")
    for b in range(N_PEERS):
        there = slice(b * HD, (b + 1) * HD)
        send_ref[:, there] = weight_ref[:, pl.ds(pl.multiple_of((2 * b + 1 - core) * HD, HD), HD)]


def slots_kernel(index_ref, out_ref):
    index = index_ref[...]
    experts = iota((ROWS, HD), 1)
    named = [index[:, k : k + 1] == experts for k in range(2)]
    both = (named[0] | named[1]).astype(BF16)
    before = (iota((ROWS, ROWS), 1) < iota((ROWS, ROWS), 0)).astype(BF16)
    earlier = dot(before, both, (1, 0))
    for k in range(2):
        slot = jnp.sum(jnp.where(named[k], earlier, 0.0), axis=1, keepdims=True).astype(jnp.int32)
        place = index[:, k : k + 1] * CAP + slot
        wide = iota((ROWS, EXPERTS * CAP), 1) == place
        out_ref[k * ROWS : (k + 1) * ROWS] = wide.astype(BF16)


def residual_kernel(grad_ref, pack_ref, onehot_ref, combine_ref, out_ref, send_ref):
    rows = pack_ref[:, :CAP].reshape(EXPERTS * CAP, HD)
    picked = dot(onehot_ref[...], rows, (1, 0))
    combine = combine_ref[...]
    moe = combine[:, 0:1] * picked[:ROWS] + combine[:, 1:2] * picked[ROWS:]
    residual = (grad_ref[...].astype(F32) + moe).astype(BF16)
    out_ref[...] = residual
    for b in range(N_PEERS):
        send_ref[b] = residual


def forward_kernel(query_ref, mate_ref, pack_ref, other_ref, probs_ref, stat_ref):
    block = lax.axis_index("zh") * 8 + lax.axis_index("y")
    query = jnp.concatenate([query_ref[...], mate_ref[...]], axis=0)
    keys, values = joined_kv(pack_ref, other_ref)
    row = iota((2 * ROWS, 1), 0) % ROWS
    number = iota((1, KEYS), 1)
    source = number % (KEYS // 2) // QUARTER
    held = half_of(number // (KEYS // 2)) * QUARTER + number % QUARTER
    allowed = position(source, key_row(held)) <= position(block, row)
    scores = jnp.where(allowed, dot(query, keys, (1, 1)) * SCALE, LOW)
    top = jnp.max(scores, axis=1, keepdims=True)
    probs = jnp.where(allowed, jnp.exp(scores - top), 0.0)
    total = jnp.sum(probs, axis=1, keepdims=True)
    probs_ref[...] = probs
    stat_ref[:, :HD] = dot(probs.astype(BF16), values, (1, 0))
    stat_ref[:, HD:] = jnp.where(iota((2 * ROWS, HD), 1) < HALF, top, total)


def project_kernel(blocks_ref, weight_ref, mate_ref, out_ref, own, seen, own_sems, seen_sems):
    core = lax.axis_index("core")
    span = 8
    own_copies = [
        pltpu.make_async_copy(
            weight_ref.at[:, pl.ds(pl.multiple_of((2 * b + core) * HD, HD), HD)],
            own.at[:, b * HD : (b + 1) * HD],
            own_sems.at[b],
        )
        for b in range(N_PEERS)
    ]
    seen_copies = [
        pltpu.make_async_copy(
            mate_ref.at[:, a * HD : (a + span) * HD],
            seen.at[:, a * HD : (a + span) * HD],
            seen_sems.at[a // span],
        )
        for a in range(0, N_PEERS, span)
    ]
    for a in range(0, N_PEERS, span):
        seen_copies[a // span].start()
        for b in range(a, a + span):
            own_copies[b].start()
    total = [jnp.zeros((ROWS, HD), F32)] * 2
    for a in range(0, N_PEERS, span):
        part = jnp.concatenate([blocks_ref[b] for b in range(a, a + span)], axis=1)
        there = slice(a * HD, (a + span) * HD)
        seen_copies[a // span].wait()
        for b in range(a, a + span):
            own_copies[b].wait()
        total = [
            total[0] + dot(part, own[:, there], (1, 1)),
            total[1] + dot(part, seen[:, there], (1, 1)),
        ]
    out_ref[:, :HD] = total[0]
    out_ref[:, HD:] = total[1]


def backward_kernel(
    part_ref, other_ref, query_ref, mate_ref, pack_ref, near_ref, probs_ref, stat_ref, seen_ref,
    kv_grad_ref, own_ref, send_ref,
):
    grad = jnp.concatenate(
        [
            part_ref[:, :HD] + other_ref[:, HD:],
            part_ref[:, HD:] + other_ref[:, :HD],
        ],
        axis=0,
    ).astype(BF16)
    query = jnp.concatenate([query_ref[...], mate_ref[...]], axis=0)
    keys, values = joined_kv(pack_ref, near_ref)
    mine = stat_ref[...]
    seen = jnp.concatenate([seen_ref[ROWS:], seen_ref[:ROWS]], axis=0)
    top_mine, top_seen = mine[:, HD : HD + 1], seen[:, HD : HD + 1]
    top = jnp.maximum(top_mine, top_seen)
    mine_gain, seen_gain = jnp.exp(top_mine - top), jnp.exp(top_seen - top)
    total = mine[:, HD + HALF : HD + HALF + 1] * mine_gain + seen[:, HD + HALF : HD + HALF + 1] * seen_gain
    mine_gain, seen_gain = mine_gain / total, seen_gain / total
    head_out = mine[:, :HD] * mine_gain + seen[:, :HD] * seen_gain
    delta = jnp.sum(grad.astype(F32) * head_out, axis=1, keepdims=True)
    probs = probs_ref[...] * mine_gain
    score_grad = (probs * (dot(grad, values, (1, 1)) - delta)).astype(BF16)
    key_grad = (dot(score_grad, query, (0, 0)) * SCALE).astype(BF16).reshape(2, 2, 8, 2, 16, HD)
    value_grad = dot(probs.astype(BF16), grad, (0, 0)).astype(BF16).reshape(2, 2, 8, 2, 16, HD)
    for part in range(2):
        half = half_of(part)
        for zh in range(2):
            there = slice(zh * 16, (zh + 1) * 16)
            kv_grad_ref[:, half, :, there, :HD] = key_grad[part, zh]
            kv_grad_ref[:, half, :, there, HD:] = value_grad[part, zh]
    query_grad = dot(score_grad, keys, (1, 0)) * SCALE
    own_ref[...] = query_grad[:ROWS]
    send_ref[...] = query_grad[ROWS:]


def sum_kernel(parts_ref, out_ref):
    total = parts_ref[0].astype(F32)
    for b in range(1, 32):
        total = total + parts_ref[b].astype(F32)
    low = total.astype(BF16)
    row, source = iota((64, 32), 0), iota((64, 32), 1)
    place = row // 4 * 2 + row % 2
    pick_key = ((place == source) & (row // 2 % 2 == 0)).astype(BF16)
    pick_value = ((place == source) & (row // 2 % 2 == 1)).astype(BF16)
    out_ref[...] = (dot(pick_key, low[:, :HD], (1, 0)) + dot(pick_value, low[:, HD:], (1, 0))).astype(BF16)


def last_kernel(parts_ref, key_ref, value_ref):
    parts = parts_ref[...].astype(F32)
    total = parts[:32] + parts[32:]
    key_ref[...] = jnp.concatenate([total[4 * g : 4 * g + 2] for g in range(8)], axis=1).astype(BF16)
    value_ref[...] = jnp.concatenate([total[4 * g + 2 : 4 * g + 4] for g in range(8)], axis=1).astype(BF16)


def swap(array):
    return lax.ppermute(array, "core", [(0, 1), (1, 0)])


def exchange(array, axes):
    return lax.all_to_all(array, axes, split_axis=0, concat_axis=0, tiled=True)


def body(out_grad, expert_rows, expert_index, combine, head_query, head_key, head_value, out_weight):
    packed = pl.pallas_call(
        pack_kernel,
        out_shape=jax.ShapeDtypeStruct((N_CTX, PACK, HD), BF16),
        in_specs=[HBM] * 3,
        out_specs=VMEM,
        scratch_shapes=[
            pltpu.VMEM((ROWS, HD), BF16),
            pltpu.VMEM((ROWS, HD), BF16),
            pltpu.SemaphoreType.DMA((3,)),
        ],
        compiler_params=PARAMS,
    )(expert_rows.reshape(N_CTX, CAP, HD), head_key, head_value)
    received = exchange(packed, CTX)
    (send_weight,) = call(weight_kernel, [((ROWS, N_PEERS * HD), BF16)], out_weight)
    mate_weight = swap(send_weight)
    mate_query = swap(head_query)
    (onehot,) = call(slots_kernel, [((2 * ROWS, EXPERTS * CAP), BF16)], expert_index)
    residual_grad, residual_send = call(
        residual_kernel,
        [((ROWS, HD), BF16), ((N_PEERS, ROWS, HD), BF16)],
        out_grad,
        received,
        onehot,
        combine,
    )
    near = lax.ppermute(received[:, CAP:], "xl", [(0, 1), (1, 0), (2, 3), (3, 2)])
    blocks = exchange(residual_send, PEERS)
    probs, stat = call(
        forward_kernel,
        [((2 * ROWS, KEYS), F32), ((2 * ROWS, 2 * HD), F32)],
        head_query,
        mate_query,
        received,
        near,
    )
    seen = swap(stat)
    part = pl.pallas_call(
        project_kernel,
        out_shape=jax.ShapeDtypeStruct((ROWS, 2 * HD), F32),
        in_specs=[VMEM, HBM, HBM],
        out_specs=VMEM,
        scratch_shapes=[
            pltpu.VMEM((ROWS, N_PEERS * HD), BF16),
            pltpu.VMEM((ROWS, N_PEERS * HD), BF16),
            pltpu.SemaphoreType.DMA((N_PEERS,)),
            pltpu.SemaphoreType.DMA((4,)),
        ],
        compiler_params=PARAMS,
    )(blocks, out_weight, mate_weight)
    other = swap(part)
    kv_grad, own_grad, send_grad = call(
        backward_kernel,
        [((8, 2, 2, 32, 2 * HD), BF16), ((ROWS, HD), F32), ((ROWS, HD), F32)],
        part,
        other,
        head_query,
        mate_query,
        received,
        near,
        probs,
        stat,
        seen,
    )
    kv_parts = exchange(kv_grad.reshape(32, 32, 2 * HD), ("y", "xl"))
    query_grad = (own_grad + swap(send_grad)).astype(BF16)
    (kv_sum,) = call(sum_kernel, [((64, HD), BF16)], kv_parts)
    final = exchange(kv_sum.reshape(16, 4, HD), ("zh", "zl", "xh"))
    key_grad, value_grad = call(
        last_kernel, [((2, 8 * HD), BF16), ((2, 8 * HD), BF16)], final.reshape(64, HD)
    )
    return residual_grad, query_grad, key_grad, value_grad


def solution(mesh):
    fine = Mesh(mesh.devices.reshape(SIZES), AXES)
    in_specs = (
        P(CTX, EXP),
        P(CTX, None, EXP),
        P(CTX, None),
        P(CTX, None),
        P(CTX, EXP),
        P(CTX, None),
        P(CTX, None),
        P(EXP, None),
    )
    out_specs = (P(CTX, EXP), P(CTX, EXP), P(CTX + EXP, None), P(CTX + EXP, None))
    return jax.shard_map(body, mesh=fine, in_specs=in_specs, out_specs=out_specs, check_vma=False)
```

```python
import math

import jax
import jax.numpy as jnp
from jax import lax
from jax.experimental import pallas as pl
from jax.experimental.pallas import tpu as pltpu
from jax.sharding import Mesh
from jax.sharding import PartitionSpec as P

HD = 128
SCALE = 1.0 / math.sqrt(HD)
LOW = -1e30
AXES = ("zh", "y", "zl", "xh", "xl", "core")
SIZES = (2, 8, 4, 2, 4, 2)
CTX = ("zh", "y")
EXP = ("zl", "xh", "xl", "core")
PEERS = ("zl", "xh", "xl")
N_CTX = 16
ROWS = 128
EXPERTS = 16
CAP = 32
N_PEERS = 32
HALF = 64
KEYS = N_CTX * HALF
QUARTER = 32
PACK = CAP + 2 * QUARTER
F32 = jnp.float32
BF16 = jnp.bfloat16
VMEM = pl.BlockSpec(memory_space=pltpu.VMEM)
HBM = pl.BlockSpec(memory_space=pltpu.HBM)
PARAMS = pltpu.CompilerParams(vmem_limit_bytes=16 * 1024 * 1024)


def in_hbm(array):
    return pltpu.with_memory_space_constraint(array, pltpu.HBM)


def call(kernel, outs, *operands, far=(), far_outs=(), scratch=()):
    return pl.pallas_call(
        kernel,
        out_shape=[
            pltpu.HBM(shape, kind) if n in far_outs else jax.ShapeDtypeStruct(shape, kind)
            for n, (shape, kind) in enumerate(outs)
        ],
        in_specs=[HBM if n in far else VMEM for n in range(len(operands))],
        out_specs=[HBM if n in far_outs else VMEM for n in range(len(outs))],
        scratch_shapes=scratch,
        compiler_params=PARAMS,
    )(*[in_hbm(operand) if n in far else operand for n, operand in enumerate(operands)])


def dot(a, b, dims):
    return lax.dot_general(a, b, ((dims[:1], dims[1:]), ((), ())), preferred_element_type=F32)


def iota(shape, dim):
    return lax.broadcasted_iota(jnp.int32, shape, dim)


def key_row(number):
    xl, zl, xh, i = number // 16, (number // 4) % 4, (number // 2) % 2, number % 2
    return zl * 32 + xh * 16 + xl * 4 + lax.axis_index("core") * 2 + i


def position(block, row):
    return jnp.where(row < 64, block, 2 * N_CTX - 1 - block) * 64 + row % 64


def half_of(part):
    mine = lax.axis_index("y") % 2
    return part + mine - 2 * part * mine


def joined_kv(pack_ref, seen_ref):
    return [
        jnp.concatenate(
            [
                pack_ref[:, CAP + at : CAP + at + QUARTER].reshape(KEYS // 2, HD),
                seen_ref[:, at : at + QUARTER].reshape(KEYS // 2, HD),
            ],
            axis=0,
        )
        for at in (0, QUARTER)
    ]


def start_all(copies):
    for copy in copies:
        copy.start()


def wait_all(copies):
    for copy in copies:
        copy.wait()


def pack_kernel(rows_ref, key_ref, value_ref, out_ref, key_own, value_own, chosen, in_sems, out_sems):
    group = lax.axis_index("zl") * 2 + lax.axis_index("xh")
    columns = pl.ds(pl.multiple_of(group * HD, HD), HD)
    rows = pltpu.make_async_copy(rows_ref, out_ref.at[:, :CAP], in_sems.at[2])
    loads = [
        pltpu.make_async_copy(key_ref.at[:, columns], key_own, in_sems.at[0]),
        pltpu.make_async_copy(value_ref.at[:, columns], value_own, in_sems.at[1]),
    ]
    start_all(loads + [rows])
    select = (iota((HALF, ROWS), 1) == key_row(iota((HALF, ROWS), 0))).astype(BF16)
    wait_all(loads)
    keys = dot(select, key_own[...], (1, 0)).astype(BF16)
    values = dot(select, value_own[...], (1, 0)).astype(BF16)
    for half in range(2):
        there = slice(half * QUARTER, (half + 1) * QUARTER)
        chosen[half, :QUARTER] = keys[there]
        chosen[half, QUARTER:] = values[there]
    stores = [
        pltpu.make_async_copy(chosen.at[c % 2], out_ref.at[c, CAP:], out_sems.at[c])
        for c in range(N_CTX)
    ]
    start_all(stores)
    wait_all(stores + [rows])


def weight_kernel(weight_ref, send_ref, sems):
    core = lax.axis_index("core")
    copies = [
        pltpu.make_async_copy(
            weight_ref.at[:, pl.ds(pl.multiple_of((2 * b + 1 - core) * HD, HD), HD)],
            send_ref.at[:, b * HD : (b + 1) * HD],
            sems.at[b],
        )
        for b in range(N_PEERS)
    ]
    start_all(copies)
    wait_all(copies)


def slots_kernel(index_ref, out_ref):
    index = index_ref[...]
    experts = iota((ROWS, HD), 1)
    named = [index[:, k : k + 1] == experts for k in range(2)]
    both = (named[0] | named[1]).astype(BF16)
    before = (iota((ROWS, ROWS), 1) < iota((ROWS, ROWS), 0)).astype(BF16)
    earlier = dot(before, both, (1, 0))
    for k in range(2):
        slot = jnp.sum(jnp.where(named[k], earlier, 0.0), axis=1, keepdims=True).astype(jnp.int32)
        place = index[:, k : k + 1] * CAP + slot
        wide = iota((ROWS, EXPERTS * CAP), 1) == place
        out_ref[k * ROWS : (k + 1) * ROWS] = wide.astype(BF16)


def residual_kernel(grad_ref, pack_ref, onehot_ref, combine_ref, out_ref, send_ref, sems):
    rows = pack_ref[:, :CAP].reshape(EXPERTS * CAP, HD)
    picked = dot(onehot_ref[...], rows, (1, 0))
    combine = combine_ref[...]
    moe = combine[:, 0:1] * picked[:ROWS] + combine[:, 1:2] * picked[ROWS:]
    out_ref[...] = (grad_ref[...].astype(F32) + moe).astype(BF16)
    copies = [pltpu.make_async_copy(out_ref, send_ref.at[b], sems.at[b]) for b in range(N_PEERS)]
    start_all(copies)
    wait_all(copies)


def forward_kernel(query_ref, mate_ref, pack_ref, other_ref, probs_ref, stat_ref):
    block = lax.axis_index("zh") * 8 + lax.axis_index("y")
    query = jnp.concatenate([query_ref[...], mate_ref[...]], axis=0)
    keys, values = joined_kv(pack_ref, other_ref)
    row = iota((2 * ROWS, 1), 0) % ROWS
    number = iota((1, KEYS), 1)
    source = number % (KEYS // 2) // QUARTER
    held = half_of(number // (KEYS // 2)) * QUARTER + number % QUARTER
    allowed = position(source, key_row(held)) <= position(block, row)
    scores = jnp.where(allowed, dot(query, keys, (1, 1)) * SCALE, LOW)
    top = jnp.max(scores, axis=1, keepdims=True)
    probs = jnp.where(allowed, jnp.exp(scores - top), 0.0)
    total = jnp.sum(probs, axis=1, keepdims=True)
    probs_ref[...] = probs
    stat_ref[:, :HD] = dot(probs.astype(BF16), values, (1, 0))
    stat_ref[:, HD:] = jnp.where(iota((2 * ROWS, HD), 1) < HALF, top, total)


def project_kernel(blocks_ref, weight_ref, mate_ref, out_ref, own, seen, own_sems, seen_sems):
    core = lax.axis_index("core")
    span = 8
    own_copies = [
        pltpu.make_async_copy(
            weight_ref.at[:, pl.ds(pl.multiple_of((2 * b + core) * HD, HD), HD)],
            own.at[:, b * HD : (b + 1) * HD],
            own_sems.at[b],
        )
        for b in range(N_PEERS)
    ]
    seen_copies = [
        pltpu.make_async_copy(
            mate_ref.at[:, a * HD : (a + span) * HD],
            seen.at[:, a * HD : (a + span) * HD],
            seen_sems.at[a // span],
        )
        for a in range(0, N_PEERS, span)
    ]
    for a in range(0, N_PEERS, span):
        seen_copies[a // span].start()
        for b in range(a, a + span):
            own_copies[b].start()
    total = [jnp.zeros((ROWS, HD), F32)] * 2
    for a in range(0, N_PEERS, span):
        part = jnp.concatenate([blocks_ref[b] for b in range(a, a + span)], axis=1)
        there = slice(a * HD, (a + span) * HD)
        seen_copies[a // span].wait()
        for b in range(a, a + span):
            own_copies[b].wait()
        total = [
            total[0] + dot(part, own[:, there], (1, 1)),
            total[1] + dot(part, seen[:, there], (1, 1)),
        ]
    out_ref[:, :HD] = total[0]
    out_ref[:, HD:] = total[1]


def backward_kernel(
    part_ref, other_ref, query_ref, mate_ref, pack_ref, near_ref, probs_ref, stat_ref, seen_ref,
    kv_grad_ref, own_ref, send_ref,
):
    grad = jnp.concatenate(
        [
            part_ref[:, :HD] + other_ref[:, HD:],
            part_ref[:, HD:] + other_ref[:, :HD],
        ],
        axis=0,
    ).astype(BF16)
    query = jnp.concatenate([query_ref[...], mate_ref[...]], axis=0)
    keys, values = joined_kv(pack_ref, near_ref)
    mine = stat_ref[...]
    seen = jnp.concatenate([seen_ref[ROWS:], seen_ref[:ROWS]], axis=0)
    top_mine, top_seen = mine[:, HD : HD + 1], seen[:, HD : HD + 1]
    top = jnp.maximum(top_mine, top_seen)
    mine_gain, seen_gain = jnp.exp(top_mine - top), jnp.exp(top_seen - top)
    total = mine[:, HD + HALF : HD + HALF + 1] * mine_gain + seen[:, HD + HALF : HD + HALF + 1] * seen_gain
    mine_gain, seen_gain = mine_gain / total, seen_gain / total
    head_out = mine[:, :HD] * mine_gain + seen[:, :HD] * seen_gain
    delta = jnp.sum(grad.astype(F32) * head_out, axis=1, keepdims=True)
    probs = probs_ref[...] * mine_gain
    score_grad = (probs * (dot(grad, values, (1, 1)) - delta)).astype(BF16)
    key_grad = (dot(score_grad, query, (0, 0)) * SCALE).astype(BF16).reshape(2, 2, 8, 2, 16, HD)
    value_grad = dot(probs.astype(BF16), grad, (0, 0)).astype(BF16).reshape(2, 2, 8, 2, 16, HD)
    for part in range(2):
        half = half_of(part)
        for zh in range(2):
            there = slice(zh * 16, (zh + 1) * 16)
            kv_grad_ref[:, half, :, there, :HD] = key_grad[part, zh]
            kv_grad_ref[:, half, :, there, HD:] = value_grad[part, zh]
    query_grad = dot(score_grad, keys, (1, 0)) * SCALE
    own_ref[...] = query_grad[:ROWS]
    send_ref[...] = query_grad[ROWS:]


def sum_kernel(parts_ref, out_ref):
    total = parts_ref[0].astype(F32)
    for b in range(1, 32):
        total = total + parts_ref[b].astype(F32)
    low = total.astype(BF16)
    row, source = iota((64, 32), 0), iota((64, 32), 1)
    place = row // 4 * 2 + row % 2
    pick_key = ((place == source) & (row // 2 % 2 == 0)).astype(BF16)
    pick_value = ((place == source) & (row // 2 % 2 == 1)).astype(BF16)
    out_ref[...] = (dot(pick_key, low[:, :HD], (1, 0)) + dot(pick_value, low[:, HD:], (1, 0))).astype(BF16)


def last_kernel(parts_ref, key_ref, value_ref):
    parts = parts_ref[...].astype(F32)
    total = parts[:32] + parts[32:]
    key_ref[...] = jnp.concatenate([total[4 * g : 4 * g + 2] for g in range(8)], axis=1).astype(BF16)
    value_ref[...] = jnp.concatenate([total[4 * g + 2 : 4 * g + 4] for g in range(8)], axis=1).astype(BF16)


def swap(array):
    return lax.ppermute(array, "core", [(0, 1), (1, 0)])


def exchange(array, axes):
    return lax.all_to_all(array, axes, split_axis=0, concat_axis=0, tiled=True)


def body(out_grad, expert_rows, expert_index, combine, head_query, head_key, head_value, out_weight):
    (packed,) = call(
        pack_kernel,
        [((N_CTX, PACK, HD), BF16)],
        expert_rows.reshape(N_CTX, CAP, HD),
        head_key,
        head_value,
        far=(0, 1, 2),
        far_outs=(0,),
        scratch=[
            pltpu.VMEM((ROWS, HD), BF16),
            pltpu.VMEM((ROWS, HD), BF16),
            pltpu.VMEM((2, 2 * QUARTER, HD), BF16),
            pltpu.SemaphoreType.DMA((3,)),
            pltpu.SemaphoreType.DMA((N_CTX,)),
        ],
    )
    received = exchange(packed, CTX)
    (send_weight,) = call(
        weight_kernel,
        [((ROWS, N_PEERS * HD), BF16)],
        out_weight,
        far=(0,),
        far_outs=(0,),
        scratch=[pltpu.SemaphoreType.DMA((N_PEERS,))],
    )
    mate_weight = swap(send_weight)
    mate_query = swap(head_query)
    (onehot,) = call(slots_kernel, [((2 * ROWS, EXPERTS * CAP), BF16)], expert_index)
    residual_grad, residual_send = call(
        residual_kernel,
        [((ROWS, HD), BF16), ((N_PEERS, ROWS, HD), BF16)],
        out_grad,
        received,
        onehot,
        combine,
        far_outs=(1,),
        scratch=[pltpu.SemaphoreType.DMA((N_PEERS,))],
    )
    near = lax.ppermute(received[:, CAP:], "y", [(n, n ^ 1) for n in range(8)])
    blocks = exchange(residual_send, PEERS)
    probs, stat = call(
        forward_kernel,
        [((2 * ROWS, KEYS), F32), ((2 * ROWS, 2 * HD), F32)],
        head_query,
        mate_query,
        received,
        near,
    )
    seen = swap(stat)
    (part,) = call(
        project_kernel,
        [((ROWS, 2 * HD), F32)],
        blocks,
        out_weight,
        mate_weight,
        far=(1, 2),
        scratch=[
            pltpu.VMEM((ROWS, N_PEERS * HD), BF16),
            pltpu.VMEM((ROWS, N_PEERS * HD), BF16),
            pltpu.SemaphoreType.DMA((N_PEERS,)),
            pltpu.SemaphoreType.DMA((4,)),
        ],
    )
    other = swap(part)
    kv_grad, own_grad, send_grad = call(
        backward_kernel,
        [((8, 2, 2, 32, 2 * HD), BF16), ((ROWS, HD), F32), ((ROWS, HD), F32)],
        part,
        other,
        head_query,
        mate_query,
        received,
        near,
        probs,
        stat,
        seen,
    )
    kv_parts = exchange(kv_grad.reshape(32, 32, 2 * HD), ("y", "xl"))
    query_grad = (own_grad + swap(send_grad)).astype(BF16)
    (kv_sum,) = call(sum_kernel, [((64, HD), BF16)], kv_parts)
    final = exchange(kv_sum.reshape(16, 4, HD), ("zh", "zl", "xh"))
    key_grad, value_grad = call(
        last_kernel, [((2, 8 * HD), BF16), ((2, 8 * HD), BF16)], final.reshape(64, HD)
    )
    return residual_grad, query_grad, key_grad, value_grad


def solution(mesh):
    fine = Mesh(mesh.devices.reshape(SIZES), AXES)
    in_specs = (
        P(CTX, EXP),
        P(CTX, None, EXP),
        P(CTX, None),
        P(CTX, None),
        P(CTX, EXP),
        P(CTX, None),
        P(CTX, None),
        P(EXP, None),
    )
    out_specs = (P(CTX, EXP), P(CTX, EXP), P(CTX + EXP, None), P(CTX + EXP, None))
    return jax.shard_map(body, mesh=fine, in_specs=in_specs, out_specs=out_specs, check_vma=False)
```

```python
import math

import jax
import jax.numpy as jnp
from jax import lax
from jax.experimental import pallas as pl
from jax.experimental.pallas import tpu as pltpu
from jax.sharding import Mesh
from jax.sharding import PartitionSpec as P

HD = 128
SCALE = 1.0 / math.sqrt(HD)
LOW = -1e30
AXES = ("zh", "y", "zl", "xh", "xl", "core")
SIZES = (2, 8, 4, 2, 4, 2)
CTX = ("zh", "y")
EXP = ("zl", "xh", "xl", "core")
PEERS = ("zl", "xh", "xl")
N_CTX = 16
ROWS = 128
EXPERTS = 16
CAP = 32
N_PEERS = 32
HALF = 64
KEYS = N_CTX * HALF
SPLIT = 2
SHARE = HALF // SPLIT
PACK = CAP + 2 * SHARE
F32 = jnp.float32
BF16 = jnp.bfloat16
VMEM = pl.BlockSpec(memory_space=pltpu.VMEM)
HBM = pl.BlockSpec(memory_space=pltpu.HBM)
PARAMS = pltpu.CompilerParams(vmem_limit_bytes=16 * 1024 * 1024)


def in_hbm(array):
    return pltpu.with_memory_space_constraint(array, pltpu.HBM)


def call(kernel, outs, *operands, far=(), far_outs=(), scratch=()):
    return pl.pallas_call(
        kernel,
        out_shape=[
            pltpu.HBM(shape, kind) if n in far_outs else jax.ShapeDtypeStruct(shape, kind)
            for n, (shape, kind) in enumerate(outs)
        ],
        in_specs=[HBM if n in far else VMEM for n in range(len(operands))],
        out_specs=[HBM if n in far_outs else VMEM for n in range(len(outs))],
        scratch_shapes=scratch,
        compiler_params=PARAMS,
    )(*[in_hbm(operand) if n in far else operand for n, operand in enumerate(operands)])


def dot(a, b, dims):
    return lax.dot_general(a, b, ((dims[:1], dims[1:]), ((), ())), preferred_element_type=F32)


def iota(shape, dim):
    return lax.broadcasted_iota(jnp.int32, shape, dim)


def key_row(number):
    xl, zl, xh, i = number // 16, (number // 4) % 4, (number // 2) % 2, number % 2
    return zl * 32 + xh * 16 + xl * 4 + lax.axis_index("core") * 2 + i


def position(block, row):
    return jnp.where(row < 64, block, 2 * N_CTX - 1 - block) * 64 + row % 64


def share_of(part):
    return lax.bitwise_xor(lax.axis_index("y") % SPLIT, part)


def joined_kv(pack_ref, *near_refs):
    return [
        jnp.concatenate(
            [pack_ref[:, CAP + at : CAP + at + SHARE].reshape(N_CTX * SHARE, HD)]
            + [near_ref[:, at : at + SHARE].reshape(N_CTX * SHARE, HD) for near_ref in near_refs],
            axis=0,
        )
        for at in (0, SHARE)
    ]


def start_all(copies):
    for copy in copies:
        copy.start()


def wait_all(copies):
    for copy in copies:
        copy.wait()


def pack_kernel(rows_ref, key_ref, value_ref, out_ref, key_own, value_own, packed, sems):
    group = lax.axis_index("zl") * 2 + lax.axis_index("xh")
    columns = pl.ds(pl.multiple_of(group * HD, HD), HD)
    rows = pltpu.make_async_copy(rows_ref, packed.at[:, :CAP], sems.at[2])
    loads = [
        pltpu.make_async_copy(key_ref.at[:, columns], key_own, sems.at[0]),
        pltpu.make_async_copy(value_ref.at[:, columns], value_own, sems.at[1]),
    ]
    start_all(loads + [rows])
    select = (iota((HALF, ROWS), 1) == key_row(iota((HALF, ROWS), 0))).astype(BF16)
    wait_all(loads)
    keys = dot(select, key_own[...], (1, 0)).astype(BF16)
    values = dot(select, value_own[...], (1, 0)).astype(BF16)
    for c in range(N_CTX):
        there = slice(c % SPLIT * SHARE, (c % SPLIT + 1) * SHARE)
        packed[c, CAP : CAP + SHARE] = keys[there]
        packed[c, CAP + SHARE :] = values[there]
    rows.wait()
    store = pltpu.make_async_copy(packed, out_ref, sems.at[3])
    store.start()
    store.wait()


def weight_kernel(weight_ref, own_ref, send_ref, whole, parted, sems):
    core = lax.axis_index("core")
    span = 8
    loads = [
        pltpu.make_async_copy(
            weight_ref.at[:, 2 * a * HD : 2 * (a + span) * HD],
            whole.at[:, 2 * a * HD : 2 * (a + span) * HD],
            sems.at[a // span],
        )
        for a in range(0, N_PEERS, span)
    ]
    start_all(loads)
    for a in range(0, N_PEERS, span):
        loads[a // span].wait()
        for b in range(a, a + span):
            there = slice(b * HD, (b + 1) * HD)
            for kind in range(2):
                column = 2 * b + (core if kind == 0 else 1 - core)
                parted[kind, :, there] = whole[:, pl.ds(pl.multiple_of(column * HD, HD), HD)]
    stores = [
        pltpu.make_async_copy(parted.at[0], own_ref, sems.at[4]),
        pltpu.make_async_copy(parted.at[1], send_ref, sems.at[5]),
    ]
    start_all(stores)
    wait_all(stores)


def slots_kernel(index_ref, out_ref):
    index = index_ref[...]
    experts = iota((ROWS, HD), 1)
    named = [index[:, k : k + 1] == experts for k in range(2)]
    both = (named[0] | named[1]).astype(BF16)
    before = (iota((ROWS, ROWS), 1) < iota((ROWS, ROWS), 0)).astype(BF16)
    earlier = dot(before, both, (1, 0))
    for k in range(2):
        slot = jnp.sum(jnp.where(named[k], earlier, 0.0), axis=1, keepdims=True).astype(jnp.int32)
        place = index[:, k : k + 1] * CAP + slot
        wide = iota((ROWS, EXPERTS * CAP), 1) == place
        out_ref[k * ROWS : (k + 1) * ROWS] = wide.astype(BF16)


def residual_kernel(grad_ref, pack_ref, onehot_ref, combine_ref, out_ref, send_ref, copied, sems):
    rows = pack_ref[:, :CAP].reshape(EXPERTS * CAP, HD)
    picked = dot(onehot_ref[...], rows, (1, 0))
    combine = combine_ref[...]
    moe = combine[:, 0:1] * picked[:ROWS] + combine[:, 1:2] * picked[ROWS:]
    residual = (grad_ref[...].astype(F32) + moe).astype(BF16)
    span = copied.shape[0]
    for b in range(span):
        copied[b] = residual
    copies = [
        pltpu.make_async_copy(copied, send_ref.at[a : a + span], sems.at[a // span])
        for a in range(0, N_PEERS, span)
    ]
    start_all(copies)
    out_ref[...] = residual
    wait_all(copies)


def forward_kernel(query_ref, mate_ref, pack_ref, *refs):
    *near_refs, probs_ref, stat_ref = refs
    block = lax.axis_index("zh") * 8 + lax.axis_index("y")
    query = jnp.concatenate([query_ref[...], mate_ref[...]], axis=0)
    keys, values = joined_kv(pack_ref, *near_refs)
    row = iota((2 * ROWS, 1), 0) % ROWS
    number = iota((1, KEYS), 1)
    source = number % (KEYS // SPLIT) // SHARE
    held = share_of(number // (KEYS // SPLIT)) * SHARE + number % SHARE
    allowed = position(source, key_row(held)) <= position(block, row)
    scores = jnp.where(allowed, dot(query, keys, (1, 1)) * SCALE, LOW)
    top = jnp.max(scores, axis=1, keepdims=True)
    probs = jnp.where(allowed, jnp.exp(scores - top), 0.0)
    total = jnp.sum(probs, axis=1, keepdims=True)
    probs_ref[...] = probs
    stat_ref[:, :HD] = dot(probs.astype(BF16), values, (1, 0))
    stat_ref[:, HD:] = jnp.where(iota((2 * ROWS, HD), 1) < HALF, top, total)


def project_kernel(blocks_ref, own_ref, mate_ref, out_ref, own, mate, sems):
    span = 8
    copies = [
        pltpu.make_async_copy(
            far.at[:, a * HD : (a + span) * HD], near.at[:, a * HD : (a + span) * HD], sems.at[k, a // span]
        )
        for a in range(0, N_PEERS, span)
        for k, (far, near) in enumerate(((own_ref, own), (mate_ref, mate)))
    ]
    start_all(copies)
    total = [jnp.zeros((ROWS, HD), F32)] * 2
    for a in range(0, N_PEERS, span):
        part = jnp.concatenate([blocks_ref[b] for b in range(a, a + span)], axis=1)
        there = slice(a * HD, (a + span) * HD)
        wait_all(copies[a // span * 2 : a // span * 2 + 2])
        total = [
            total[0] + dot(part, own[:, there], (1, 1)),
            total[1] + dot(part, mate[:, there], (1, 1)),
        ]
    out_ref[:, :HD] = total[0]
    out_ref[:, HD:] = total[1]


def backward_kernel(
    part_ref, other_ref, query_ref, mate_ref, probs_ref, stat_ref, seen_ref, pack_ref, *refs
):
    *near_refs, kv_grad_ref, own_ref, send_ref = refs
    grad = jnp.concatenate(
        [
            part_ref[:, :HD] + other_ref[:, HD:],
            part_ref[:, HD:] + other_ref[:, :HD],
        ],
        axis=0,
    ).astype(BF16)
    query = jnp.concatenate([query_ref[...], mate_ref[...]], axis=0)
    keys, values = joined_kv(pack_ref, *near_refs)
    mine = stat_ref[...]
    seen = jnp.concatenate([seen_ref[ROWS:], seen_ref[:ROWS]], axis=0)
    top_mine, top_seen = mine[:, HD : HD + 1], seen[:, HD : HD + 1]
    top = jnp.maximum(top_mine, top_seen)
    mine_gain, seen_gain = jnp.exp(top_mine - top), jnp.exp(top_seen - top)
    total = mine[:, HD + HALF : HD + HALF + 1] * mine_gain + seen[:, HD + HALF : HD + HALF + 1] * seen_gain
    mine_gain, seen_gain = mine_gain / total, seen_gain / total
    head_out = mine[:, :HD] * mine_gain + seen[:, :HD] * seen_gain
    delta = jnp.sum(grad.astype(F32) * head_out, axis=1, keepdims=True)
    probs = probs_ref[...] * mine_gain
    score_grad = (probs * (dot(grad, values, (1, 1)) - delta)).astype(BF16)
    shape = (SPLIT, 2, 8, 4 // SPLIT, 16, HD)
    key_grad = (dot(score_grad, query, (0, 0)) * SCALE).astype(BF16).reshape(shape)
    value_grad = dot(probs.astype(BF16), grad, (0, 0)).astype(BF16).reshape(shape)
    for part in range(SPLIT):
        share = share_of(part)
        for zh in range(2):
            there = slice(zh * 16, (zh + 1) * 16)
            kv_grad_ref[:, share, :, there, :HD] = key_grad[part, zh]
            kv_grad_ref[:, share, :, there, HD:] = value_grad[part, zh]
    query_grad = dot(score_grad, keys, (1, 0)) * SCALE
    own_ref[...] = query_grad[:ROWS]
    send_ref[...] = query_grad[ROWS:]


def sum_kernel(parts_ref, out_ref):
    total = parts_ref[0].astype(F32)
    for b in range(1, 32):
        total = total + parts_ref[b].astype(F32)
    low = total.astype(BF16)
    row, source = iota((64, 32), 0), iota((64, 32), 1)
    place = row // 4 * 2 + row % 2
    pick_key = ((place == source) & (row // 2 % 2 == 0)).astype(BF16)
    pick_value = ((place == source) & (row // 2 % 2 == 1)).astype(BF16)
    out_ref[...] = (dot(pick_key, low[:, :HD], (1, 0)) + dot(pick_value, low[:, HD:], (1, 0))).astype(BF16)


def last_kernel(parts_ref, key_ref, value_ref):
    parts = parts_ref[...].astype(F32)
    total = parts[:32] + parts[32:]
    key_ref[...] = jnp.concatenate([total[4 * g : 4 * g + 2] for g in range(8)], axis=1).astype(BF16)
    value_ref[...] = jnp.concatenate([total[4 * g + 2 : 4 * g + 4] for g in range(8)], axis=1).astype(BF16)


def swap(array):
    return lax.ppermute(array, "core", [(0, 1), (1, 0)])


def exchange(array, axes):
    return lax.all_to_all(array, axes, split_axis=0, concat_axis=0, tiled=True)


def body(out_grad, expert_rows, expert_index, combine, head_query, head_key, head_value, out_weight):
    (packed,) = call(
        pack_kernel,
        [((N_CTX, PACK, HD), BF16)],
        expert_rows.reshape(N_CTX, CAP, HD),
        head_key,
        head_value,
        far=(0, 1, 2),
        far_outs=(0,),
        scratch=[
            pltpu.VMEM((ROWS, HD), BF16),
            pltpu.VMEM((ROWS, HD), BF16),
            pltpu.VMEM((N_CTX, PACK, HD), BF16),
            pltpu.SemaphoreType.DMA((4,)),
        ],
    )
    received = exchange(packed, CTX)
    own_weight, send_weight = call(
        weight_kernel,
        [((ROWS, N_PEERS * HD), BF16)] * 2,
        out_weight,
        far=(0,),
        far_outs=(0, 1),
        scratch=[
            pltpu.VMEM((ROWS, 2 * N_PEERS * HD), BF16),
            pltpu.VMEM((2, ROWS, N_PEERS * HD), BF16),
            pltpu.SemaphoreType.DMA((6,)),
        ],
    )
    mate_weight = swap(send_weight)
    mate_query = swap(head_query)
    (onehot,) = call(slots_kernel, [((2 * ROWS, EXPERTS * CAP), BF16)], expert_index)
    residual_grad, residual_send = call(
        residual_kernel,
        [((ROWS, HD), BF16), ((N_PEERS, ROWS, HD), BF16)],
        out_grad,
        received,
        onehot,
        combine,
        far_outs=(1,),
        scratch=[pltpu.VMEM((8, ROWS, HD), BF16), pltpu.SemaphoreType.DMA((4,))],
    )
    held = received[:, CAP:]
    near = [lax.ppermute(held, "y", [(n, n ^ p) for n in range(8)]) for p in range(1, SPLIT)]
    blocks = exchange(residual_send, PEERS)
    probs, stat = call(
        forward_kernel,
        [((2 * ROWS, KEYS), F32), ((2 * ROWS, 2 * HD), F32)],
        head_query,
        mate_query,
        received,
        *near,
    )
    seen = swap(stat)
    (part,) = call(
        project_kernel,
        [((ROWS, 2 * HD), F32)],
        blocks,
        own_weight,
        mate_weight,
        far=(1, 2),
        scratch=[
            pltpu.VMEM((ROWS, N_PEERS * HD), BF16),
            pltpu.VMEM((ROWS, N_PEERS * HD), BF16),
            pltpu.SemaphoreType.DMA((2, 4)),
        ],
    )
    other = swap(part)
    kv_grad, own_grad, send_grad = call(
        backward_kernel,
        [((8, SPLIT, 4 // SPLIT, 32, 2 * HD), BF16), ((ROWS, HD), F32), ((ROWS, HD), F32)],
        part,
        other,
        head_query,
        mate_query,
        probs,
        stat,
        seen,
        received,
        *near,
    )
    kv_parts = exchange(kv_grad.reshape(32, 32, 2 * HD), ("y", "xl"))
    query_grad = (own_grad + swap(send_grad)).astype(BF16)
    (kv_sum,) = call(sum_kernel, [((64, HD), BF16)], kv_parts)
    final = exchange(kv_sum.reshape(16, 4, HD), ("zh", "zl", "xh"))
    key_grad, value_grad = call(
        last_kernel, [((2, 8 * HD), BF16), ((2, 8 * HD), BF16)], final.reshape(64, HD)
    )
    return residual_grad, query_grad, key_grad, value_grad


def solution(mesh):
    fine = Mesh(mesh.devices.reshape(SIZES), AXES)
    in_specs = (
        P(CTX, EXP),
        P(CTX, None, EXP),
        P(CTX, None),
        P(CTX, None),
        P(CTX, EXP),
        P(CTX, None),
        P(CTX, None),
        P(EXP, None),
    )
    out_specs = (P(CTX, EXP), P(CTX, EXP), P(CTX + EXP, None), P(CTX + EXP, None))
    return jax.shard_map(body, mesh=fine, in_specs=in_specs, out_specs=out_specs, check_vma=False)
```

```python
import math

import jax
import jax.numpy as jnp
from jax import lax
from jax.experimental import pallas as pl
from jax.experimental.pallas import tpu as pltpu
from jax.sharding import Mesh
from jax.sharding import PartitionSpec as P

HD = 128
SCALE = 1.0 / math.sqrt(HD)
LOW = -1e30
AXES = ("zh", "y", "zl", "xh", "xl", "core")
SIZES = (2, 8, 4, 2, 4, 2)
CTX = ("zh", "y")
EXP = ("zl", "xh", "xl", "core")
PEERS = ("zl", "xh", "xl")
N_CTX = 16
ROWS = 128
EXPERTS = 16
CAP = 32
N_PEERS = 32
HALF = 64
KEYS = N_CTX * HALF
SPLIT = 4
SHARE = HALF // SPLIT
PACK = CAP + 2 * SHARE
F32 = jnp.float32
BF16 = jnp.bfloat16
VMEM = pl.BlockSpec(memory_space=pltpu.VMEM)
HBM = pl.BlockSpec(memory_space=pltpu.HBM)
PARAMS = pltpu.CompilerParams(vmem_limit_bytes=16 * 1024 * 1024)


def in_hbm(array):
    return pltpu.with_memory_space_constraint(array, pltpu.HBM)


def call(kernel, outs, *operands, far=(), free=(), far_outs=(), scratch=()):
    spaces = {n: HBM for n in far} | {n: pl.BlockSpec(memory_space=pl.ANY) for n in free}
    return pl.pallas_call(
        kernel,
        out_shape=[
            pltpu.HBM(shape, kind) if n in far_outs else jax.ShapeDtypeStruct(shape, kind)
            for n, (shape, kind) in enumerate(outs)
        ],
        in_specs=[spaces.get(n, VMEM) for n in range(len(operands))],
        out_specs=[HBM if n in far_outs else VMEM for n in range(len(outs))],
        scratch_shapes=scratch,
        compiler_params=PARAMS,
    )(*[in_hbm(operand) if n in far else operand for n, operand in enumerate(operands)])


def dot(a, b, dims):
    return lax.dot_general(a, b, ((dims[:1], dims[1:]), ((), ())), preferred_element_type=F32)


def iota(shape, dim):
    return lax.broadcasted_iota(jnp.int32, shape, dim)


def key_row(number):
    xl, zl, xh, i = number // 16, (number // 4) % 4, (number // 2) % 2, number % 2
    return zl * 32 + xh * 16 + xl * 4 + lax.axis_index("core") * 2 + i


def position(block, row):
    return jnp.where(row < 64, block, 2 * N_CTX - 1 - block) * 64 + row % 64


def share_of(part):
    return lax.bitwise_xor(lax.axis_index("y") % SPLIT, part)


def joined_kv(pack_ref, *near_refs):
    return [
        jnp.concatenate(
            [pack_ref[:, CAP + at : CAP + at + SHARE].reshape(N_CTX * SHARE, HD)]
            + [near_ref[:, at : at + SHARE].reshape(N_CTX * SHARE, HD) for near_ref in near_refs],
            axis=0,
        )
        for at in (0, SHARE)
    ]


def start_all(copies):
    for copy in copies:
        copy.start()


def wait_all(copies):
    for copy in copies:
        copy.wait()


def pack_kernel(rows_ref, key_ref, value_ref, out_ref, key_own, value_own, packed, sems):
    group = lax.axis_index("zl") * 2 + lax.axis_index("xh")
    columns = pl.ds(pl.multiple_of(group * HD, HD), HD)
    rows = pltpu.make_async_copy(rows_ref, packed.at[:, :CAP], sems.at[2])
    loads = [
        pltpu.make_async_copy(key_ref.at[:, columns], key_own, sems.at[0]),
        pltpu.make_async_copy(value_ref.at[:, columns], value_own, sems.at[1]),
    ]
    start_all(loads + [rows])
    select = (iota((HALF, ROWS), 1) == key_row(iota((HALF, ROWS), 0))).astype(BF16)
    wait_all(loads)
    keys = dot(select, key_own[...], (1, 0)).astype(BF16)
    values = dot(select, value_own[...], (1, 0)).astype(BF16)
    for c in range(N_CTX):
        there = slice(c % SPLIT * SHARE, (c % SPLIT + 1) * SHARE)
        packed[c, CAP : CAP + SHARE] = keys[there]
        packed[c, CAP + SHARE :] = values[there]
    rows.wait()
    store = pltpu.make_async_copy(packed, out_ref, sems.at[3])
    store.start()
    store.wait()


def weight_kernel(weight_ref, own_ref, send_ref, token_ref, whole, parted, sems):
    core = lax.axis_index("core")
    span = 8
    loads = [
        pltpu.make_async_copy(
            weight_ref.at[:, 2 * a * HD : 2 * (a + span) * HD],
            whole.at[:, 2 * a * HD : 2 * (a + span) * HD],
            sems.at[a // span],
        )
        for a in range(0, N_PEERS, span)
    ]
    start_all(loads)
    for a in range(0, N_PEERS, span):
        loads[a // span].wait()
        for b in range(a, a + span):
            there = slice(b * HD, (b + 1) * HD)
            for kind in range(2):
                column = 2 * b + (core if kind == 0 else 1 - core)
                parted[kind, :, there] = whole[:, pl.ds(pl.multiple_of(column * HD, HD), HD)]
    stores = [
        pltpu.make_async_copy(parted.at[0], own_ref, sems.at[4]),
        pltpu.make_async_copy(parted.at[1], send_ref, sems.at[5]),
    ]
    start_all(stores)
    token_ref[...] = jnp.zeros_like(token_ref)
    wait_all(stores)


def slots_kernel(index_ref, out_ref):
    index = index_ref[...]
    experts = iota((ROWS, HD), 1)
    named = [index[:, k : k + 1] == experts for k in range(2)]
    both = (named[0] | named[1]).astype(BF16)
    before = (iota((ROWS, ROWS), 1) < iota((ROWS, ROWS), 0)).astype(BF16)
    earlier = dot(before, both, (1, 0))
    for k in range(2):
        slot = jnp.sum(jnp.where(named[k], earlier, 0.0), axis=1, keepdims=True).astype(jnp.int32)
        place = index[:, k : k + 1] * CAP + slot
        wide = iota((ROWS, EXPERTS * CAP), 1) == place
        out_ref[k * ROWS : (k + 1) * ROWS] = wide.astype(BF16)


def residual_kernel(
    grad_ref, pack_ref, onehot_ref, combine_ref, _token, out_ref, send_ref, copied, sems
):
    rows = pack_ref[:, :CAP].reshape(EXPERTS * CAP, HD)
    picked = dot(onehot_ref[...], rows, (1, 0))
    combine = combine_ref[...]
    moe = combine[:, 0:1] * picked[:ROWS] + combine[:, 1:2] * picked[ROWS:]
    residual = (grad_ref[...].astype(F32) + moe).astype(BF16)
    span = 8
    copies = []
    for a in range(0, N_PEERS, span):
        for b in range(a, a + span):
            copied[b] = residual
        copy = pltpu.make_async_copy(
            copied.at[a : a + span], send_ref.at[a : a + span], sems.at[a // span]
        )
        copy.start()
        copies.append(copy)
    out_ref[...] = residual
    wait_all(copies)


def forward_kernel(query_ref, mate_ref, pack_ref, *refs):
    *near_refs, probs_ref, stat_ref = refs
    block = lax.axis_index("zh") * 8 + lax.axis_index("y")
    query = jnp.concatenate([query_ref[...], mate_ref[...]], axis=0)
    keys, values = joined_kv(pack_ref, *near_refs)
    row = iota((2 * ROWS, 1), 0) % ROWS
    number = iota((1, KEYS), 1)
    source = number % (KEYS // SPLIT) // SHARE
    held = share_of(number // (KEYS // SPLIT)) * SHARE + number % SHARE
    allowed = position(source, key_row(held)) <= position(block, row)
    scores = jnp.where(allowed, dot(query, keys, (1, 1)) * SCALE, LOW)
    top = jnp.max(scores, axis=1, keepdims=True)
    probs = jnp.where(allowed, jnp.exp(scores - top), 0.0)
    total = jnp.sum(probs, axis=1, keepdims=True)
    probs_ref[...] = probs
    stat_ref[:, :HD] = dot(probs.astype(BF16), values, (1, 0))
    stat_ref[:, HD:] = jnp.where(iota((2 * ROWS, HD), 1) < HALF, top, total)


def project_kernel(blocks_ref, own_ref, mate_ref, out_ref, own, mate, sems):
    span = 8
    copies = [
        pltpu.make_async_copy(
            far.at[:, a * HD : (a + span) * HD], near.at[:, a * HD : (a + span) * HD], sems.at[k, a // span]
        )
        for a in range(0, N_PEERS, span)
        for k, (far, near) in enumerate(((own_ref, own), (mate_ref, mate)))
    ]
    start_all(copies)
    total = [jnp.zeros((ROWS, HD), F32)] * 2
    for a in range(0, N_PEERS, span):
        part = jnp.concatenate([blocks_ref[b] for b in range(a, a + span)], axis=1)
        there = slice(a * HD, (a + span) * HD)
        wait_all(copies[a // span * 2 : a // span * 2 + 2])
        total = [
            total[0] + dot(part, own[:, there], (1, 1)),
            total[1] + dot(part, mate[:, there], (1, 1)),
        ]
    out_ref[:, :HD] = total[0]
    out_ref[:, HD:] = total[1]


def backward_kernel(
    part_ref, other_ref, query_ref, mate_ref, probs_ref, stat_ref, seen_ref, pack_ref, *refs
):
    *near_refs, kv_grad_ref, own_ref, send_ref = refs
    grad = jnp.concatenate(
        [
            part_ref[:, :HD] + other_ref[:, HD:],
            part_ref[:, HD:] + other_ref[:, :HD],
        ],
        axis=0,
    ).astype(BF16)
    query = jnp.concatenate([query_ref[...], mate_ref[...]], axis=0)
    keys, values = joined_kv(pack_ref, *near_refs)
    mine = stat_ref[...]
    seen = jnp.concatenate([seen_ref[ROWS:], seen_ref[:ROWS]], axis=0)
    top_mine, top_seen = mine[:, HD : HD + 1], seen[:, HD : HD + 1]
    top = jnp.maximum(top_mine, top_seen)
    mine_gain, seen_gain = jnp.exp(top_mine - top), jnp.exp(top_seen - top)
    total = mine[:, HD + HALF : HD + HALF + 1] * mine_gain + seen[:, HD + HALF : HD + HALF + 1] * seen_gain
    mine_gain, seen_gain = mine_gain / total, seen_gain / total
    head_out = mine[:, :HD] * mine_gain + seen[:, :HD] * seen_gain
    delta = jnp.sum(grad.astype(F32) * head_out, axis=1, keepdims=True)
    probs = probs_ref[...] * mine_gain
    score_grad = (probs * (dot(grad, values, (1, 1)) - delta)).astype(BF16)
    shape = (SPLIT, 2, 8, 4 // SPLIT, 16, HD)
    key_grad = (dot(score_grad, query, (0, 0)) * SCALE).astype(BF16).reshape(shape)
    value_grad = dot(probs.astype(BF16), grad, (0, 0)).astype(BF16).reshape(shape)
    for part in range(SPLIT):
        share = share_of(part)
        for zh in range(2):
            there = slice(zh * 16, (zh + 1) * 16)
            kv_grad_ref[:, share, :, there, :HD] = key_grad[part, zh]
            kv_grad_ref[:, share, :, there, HD:] = value_grad[part, zh]
    query_grad = dot(score_grad, keys, (1, 0)) * SCALE
    own_ref[...] = query_grad[:ROWS]
    send_ref[...] = query_grad[ROWS:]


def sum_kernel(parts_ref, out_ref):
    total = parts_ref[0].astype(F32)
    for b in range(1, 32):
        total = total + parts_ref[b].astype(F32)
    low = total.astype(BF16)
    row, source = iota((64, 32), 0), iota((64, 32), 1)
    place = row // 4 * 2 + row % 2
    pick_key = ((place == source) & (row // 2 % 2 == 0)).astype(BF16)
    pick_value = ((place == source) & (row // 2 % 2 == 1)).astype(BF16)
    out_ref[...] = (dot(pick_key, low[:, :HD], (1, 0)) + dot(pick_value, low[:, HD:], (1, 0))).astype(BF16)


def last_kernel(parts_ref, key_ref, value_ref):
    parts = parts_ref[...].astype(F32)
    total = parts[:32] + parts[32:]
    key_ref[...] = jnp.concatenate([total[4 * g : 4 * g + 2] for g in range(8)], axis=1).astype(BF16)
    value_ref[...] = jnp.concatenate([total[4 * g + 2 : 4 * g + 4] for g in range(8)], axis=1).astype(BF16)


def swap(array):
    return lax.ppermute(array, "core", [(0, 1), (1, 0)])


def exchange(array, axes):
    return lax.all_to_all(array, axes, split_axis=0, concat_axis=0, tiled=True)


def body(out_grad, expert_rows, expert_index, combine, head_query, head_key, head_value, out_weight):
    (packed,) = call(
        pack_kernel,
        [((N_CTX, PACK, HD), BF16)],
        expert_rows.reshape(N_CTX, CAP, HD),
        head_key,
        head_value,
        far=(0, 1, 2),
        far_outs=(0,),
        scratch=[
            pltpu.VMEM((ROWS, HD), BF16),
            pltpu.VMEM((ROWS, HD), BF16),
            pltpu.VMEM((N_CTX, PACK, HD), BF16),
            pltpu.SemaphoreType.DMA((4,)),
        ],
    )
    received = exchange(packed, CTX)
    own_weight, send_weight, token = call(
        weight_kernel,
        [((ROWS, N_PEERS * HD), BF16)] * 2 + [((8, HD), F32)],
        out_weight,
        far=(0,),
        far_outs=(0, 1),
        scratch=[
            pltpu.VMEM((ROWS, 2 * N_PEERS * HD), BF16),
            pltpu.VMEM((2, ROWS, N_PEERS * HD), BF16),
            pltpu.SemaphoreType.DMA((6,)),
        ],
    )
    mate_weight = swap(send_weight)
    mate_query = swap(head_query)
    (onehot,) = call(slots_kernel, [((2 * ROWS, EXPERTS * CAP), BF16)], expert_index)
    residual_grad, residual_send = call(
        residual_kernel,
        [((ROWS, HD), BF16), ((N_PEERS, ROWS, HD), BF16)],
        out_grad,
        received,
        onehot,
        combine,
        token,
        free=(4,),
        far_outs=(1,),
        scratch=[pltpu.VMEM((N_PEERS, ROWS, HD), BF16), pltpu.SemaphoreType.DMA((4,))],
    )
    held = received[:, CAP:]
    near = [lax.ppermute(held, "y", [(n, n ^ p) for n in range(8)]) for p in range(1, SPLIT)]
    blocks = exchange(residual_send, PEERS)
    probs, stat = call(
        forward_kernel,
        [((2 * ROWS, KEYS), F32), ((2 * ROWS, 2 * HD), F32)],
        head_query,
        mate_query,
        received,
        *near,
    )
    seen = swap(stat)
    (part,) = call(
        project_kernel,
        [((ROWS, 2 * HD), F32)],
        blocks,
        own_weight,
        mate_weight,
        far=(1, 2),
        scratch=[
            pltpu.VMEM((ROWS, N_PEERS * HD), BF16),
            pltpu.VMEM((ROWS, N_PEERS * HD), BF16),
            pltpu.SemaphoreType.DMA((2, 4)),
        ],
    )
    other = swap(part)
    kv_grad, own_grad, send_grad = call(
        backward_kernel,
        [((8, SPLIT, 4 // SPLIT, 32, 2 * HD), BF16), ((ROWS, HD), F32), ((ROWS, HD), F32)],
        part,
        other,
        head_query,
        mate_query,
        probs,
        stat,
        seen,
        received,
        *near,
    )
    kv_parts = exchange(kv_grad.reshape(32, 32, 2 * HD), ("y", "xl"))
    query_grad = (own_grad + swap(send_grad)).astype(BF16)
    (kv_sum,) = call(sum_kernel, [((64, HD), BF16)], kv_parts)
    final = exchange(kv_sum.reshape(16, 4, HD), ("zh", "zl", "xh"))
    key_grad, value_grad = call(
        last_kernel, [((2, 8 * HD), BF16), ((2, 8 * HD), BF16)], final.reshape(64, HD)
    )
    return residual_grad, query_grad, key_grad, value_grad


def solution(mesh):
    fine = Mesh(mesh.devices.reshape(SIZES), AXES)
    in_specs = (
        P(CTX, EXP),
        P(CTX, None, EXP),
        P(CTX, None),
        P(CTX, None),
        P(CTX, EXP),
        P(CTX, None),
        P(CTX, None),
        P(EXP, None),
    )
    out_specs = (P(CTX, EXP), P(CTX, EXP), P(CTX + EXP, None), P(CTX + EXP, None))
    return jax.shard_map(body, mesh=fine, in_specs=in_specs, out_specs=out_specs, check_vma=False)
```

```python
import math

import jax
import jax.numpy as jnp
from jax import lax
from jax.experimental import pallas as pl
from jax.experimental.pallas import tpu as pltpu
from jax.sharding import Mesh
from jax.sharding import PartitionSpec as P

HD = 128
SCALE = 1.0 / math.sqrt(HD)
LOW = -1e30
AXES = ("zh", "y", "zl", "xh", "xl", "core")
SIZES = (2, 8, 4, 2, 4, 2)
CTX = ("zh", "y")
EXP = ("zl", "xh", "xl", "core")
PEERS = ("zl", "xh", "xl")
N_CTX = 16
ROWS = 128
EXPERTS = 16
CAP = 32
N_PEERS = 32
HALF = 64
KEYS = N_CTX * HALF
SPAN = 8
CHUNKS = N_PEERS // SPAN
WEIGHTS = (CHUNKS, ROWS, SPAN * HD)
SPLIT = 4
SHARE = HALF // SPLIT
PACK = CAP + 2 * SHARE
F32 = jnp.float32
BF16 = jnp.bfloat16
VMEM = pl.BlockSpec(memory_space=pltpu.VMEM)
HBM = pl.BlockSpec(memory_space=pltpu.HBM)
PARAMS = pltpu.CompilerParams(vmem_limit_bytes=16 * 1024 * 1024)


def in_hbm(array):
    return pltpu.with_memory_space_constraint(array, pltpu.HBM)


def call(kernel, outs, *operands, far=(), free=(), far_outs=(), scratch=()):
    spaces = {n: HBM for n in far} | {n: pl.BlockSpec(memory_space=pl.ANY) for n in free}
    return pl.pallas_call(
        kernel,
        out_shape=[
            pltpu.HBM(shape, kind) if n in far_outs else jax.ShapeDtypeStruct(shape, kind)
            for n, (shape, kind) in enumerate(outs)
        ],
        in_specs=[spaces.get(n, VMEM) for n in range(len(operands))],
        out_specs=[HBM if n in far_outs else VMEM for n in range(len(outs))],
        scratch_shapes=scratch,
        compiler_params=PARAMS,
    )(*[in_hbm(operand) if n in far else operand for n, operand in enumerate(operands)])


def dot(a, b, dims):
    return lax.dot_general(a, b, ((dims[:1], dims[1:]), ((), ())), preferred_element_type=F32)


def iota(shape, dim):
    return lax.broadcasted_iota(jnp.int32, shape, dim)


def key_row(number):
    xl, zl, xh, i = number // 16, (number // 4) % 4, (number // 2) % 2, number % 2
    return zl * 32 + xh * 16 + xl * 4 + lax.axis_index("core") * 2 + i


def position(block, row):
    return jnp.where(row < 64, block, 2 * N_CTX - 1 - block) * 64 + row % 64


def share_of(part):
    return lax.bitwise_xor(lax.axis_index("y") % SPLIT, part)


def joined_kv(pack_ref, *near_refs):
    return [
        jnp.concatenate(
            [pack_ref[:, CAP + at : CAP + at + SHARE].reshape(N_CTX * SHARE, HD)]
            + [near_ref[:, at : at + SHARE].reshape(N_CTX * SHARE, HD) for near_ref in near_refs],
            axis=0,
        )
        for at in (0, SHARE)
    ]


def start_all(copies):
    for copy in copies:
        copy.start()


def wait_all(copies):
    for copy in copies:
        copy.wait()


def pack_kernel(rows_ref, key_ref, value_ref, out_ref, key_own, value_own, packed, sems):
    group = lax.axis_index("zl") * 2 + lax.axis_index("xh")
    columns = pl.ds(pl.multiple_of(group * HD, HD), HD)
    rows = pltpu.make_async_copy(rows_ref, packed.at[:, :CAP], sems.at[2])
    loads = [
        pltpu.make_async_copy(key_ref.at[:, columns], key_own, sems.at[0]),
        pltpu.make_async_copy(value_ref.at[:, columns], value_own, sems.at[1]),
    ]
    start_all(loads + [rows])
    select = (iota((HALF, ROWS), 1) == key_row(iota((HALF, ROWS), 0))).astype(BF16)
    wait_all(loads)
    keys = dot(select, key_own[...], (1, 0)).astype(BF16)
    values = dot(select, value_own[...], (1, 0)).astype(BF16)
    for c in range(N_CTX):
        there = slice(c % SPLIT * SHARE, (c % SPLIT + 1) * SHARE)
        packed[c, CAP : CAP + SHARE] = keys[there]
        packed[c, CAP + SHARE :] = values[there]
    rows.wait()
    store = pltpu.make_async_copy(packed, out_ref, sems.at[3])
    store.start()
    store.wait()


def weight_kernel(weight_ref, own_ref, send_ref, token_ref, whole, own, send, sems):
    core = lax.axis_index("core")
    wide = 2 * SPAN * HD
    loads = [
        pltpu.make_async_copy(
            weight_ref.at[:, k * wide : (k + 1) * wide], whole.at[:, k * wide : (k + 1) * wide], sems.at[k]
        )
        for k in range(CHUNKS)
    ]
    start_all(loads)
    for k in range(CHUNKS):
        loads[k].wait()
        for b in range(SPAN):
            column = 2 * (k * SPAN + b)
            there = slice(b * HD, (b + 1) * HD)
            own[k, :, there] = whole[:, pl.ds(pl.multiple_of((column + core) * HD, HD), HD)]
            send[k, :, there] = whole[:, pl.ds(pl.multiple_of((column + 1 - core) * HD, HD), HD)]
    stores = [
        pltpu.make_async_copy(own, own_ref, sems.at[CHUNKS]),
        pltpu.make_async_copy(send, send_ref, sems.at[CHUNKS + 1]),
    ]
    start_all(stores)
    token_ref[...] = jnp.zeros_like(token_ref)
    wait_all(stores)


def slots_kernel(index_ref, out_ref):
    index = index_ref[...]
    experts = iota((ROWS, HD), 1)
    named = [index[:, k : k + 1] == experts for k in range(2)]
    both = (named[0] | named[1]).astype(BF16)
    before = (iota((ROWS, ROWS), 1) < iota((ROWS, ROWS), 0)).astype(BF16)
    earlier = dot(before, both, (1, 0))
    for k in range(2):
        slot = jnp.sum(jnp.where(named[k], earlier, 0.0), axis=1, keepdims=True).astype(jnp.int32)
        place = index[:, k : k + 1] * CAP + slot
        wide = iota((ROWS, EXPERTS * CAP), 1) == place
        out_ref[k * ROWS : (k + 1) * ROWS] = wide.astype(BF16)


def residual_kernel(
    grad_ref, pack_ref, onehot_ref, combine_ref, _token, out_ref, send_ref, copied, sems
):
    rows = pack_ref[:, :CAP].reshape(EXPERTS * CAP, HD)
    picked = dot(onehot_ref[...], rows, (1, 0))
    combine = combine_ref[...]
    moe = combine[:, 0:1] * picked[:ROWS] + combine[:, 1:2] * picked[ROWS:]
    residual = (grad_ref[...].astype(F32) + moe).astype(BF16)
    span = 8
    copies = []
    for a in range(0, N_PEERS, span):
        for b in range(a, a + span):
            copied[b] = residual
        copy = pltpu.make_async_copy(
            copied.at[a : a + span], send_ref.at[a : a + span], sems.at[a // span]
        )
        copy.start()
        copies.append(copy)
    out_ref[...] = residual
    wait_all(copies)


def forward_kernel(query_ref, mate_ref, pack_ref, *refs):
    *near_refs, probs_ref, stat_ref = refs
    block = lax.axis_index("zh") * 8 + lax.axis_index("y")
    query = jnp.concatenate([query_ref[...], mate_ref[...]], axis=0)
    keys, values = joined_kv(pack_ref, *near_refs)
    row = iota((2 * ROWS, 1), 0) % ROWS
    number = iota((1, KEYS), 1)
    source = number % (KEYS // SPLIT) // SHARE
    held = share_of(number // (KEYS // SPLIT)) * SHARE + number % SHARE
    allowed = position(source, key_row(held)) <= position(block, row)
    scores = jnp.where(allowed, dot(query, keys, (1, 1)) * SCALE, LOW)
    top = jnp.max(scores, axis=1, keepdims=True)
    probs = jnp.where(allowed, jnp.exp(scores - top), 0.0)
    total = jnp.sum(probs, axis=1, keepdims=True)
    probs_ref[...] = probs
    stat_ref[:, :HD] = dot(probs.astype(BF16), values, (1, 0))
    stat_ref[:, HD:] = jnp.where(iota((2 * ROWS, HD), 1) < HALF, top, total)


def project_kernel(blocks_ref, own_ref, mate_ref, out_ref, own, mate, sems):
    copies = [
        pltpu.make_async_copy(far.at[k], near.at[k], sems.at[kind, k])
        for k in range(CHUNKS)
        for kind, (far, near) in enumerate(((own_ref, own), (mate_ref, mate)))
    ]
    start_all(copies)
    total = [jnp.zeros((ROWS, HD), F32)] * 2
    for k in range(CHUNKS):
        part = jnp.concatenate([blocks_ref[b] for b in range(k * SPAN, (k + 1) * SPAN)], axis=1)
        wait_all(copies[2 * k : 2 * k + 2])
        total = [total[0] + dot(part, own[k], (1, 1)), total[1] + dot(part, mate[k], (1, 1))]
    out_ref[:, :HD] = total[0]
    out_ref[:, HD:] = total[1]


def backward_kernel(
    part_ref, other_ref, query_ref, mate_ref, probs_ref, stat_ref, seen_ref, pack_ref, *refs
):
    *near_refs, kv_grad_ref, own_ref, send_ref, staged, sems = refs
    grad = jnp.concatenate(
        [
            part_ref[:, :HD] + other_ref[:, HD:],
            part_ref[:, HD:] + other_ref[:, :HD],
        ],
        axis=0,
    ).astype(BF16)
    query = jnp.concatenate([query_ref[...], mate_ref[...]], axis=0)
    keys, values = joined_kv(pack_ref, *near_refs)
    mine = stat_ref[...]
    seen = jnp.concatenate([seen_ref[ROWS:], seen_ref[:ROWS]], axis=0)
    top_mine, top_seen = mine[:, HD : HD + 1], seen[:, HD : HD + 1]
    top = jnp.maximum(top_mine, top_seen)
    mine_gain, seen_gain = jnp.exp(top_mine - top), jnp.exp(top_seen - top)
    total = mine[:, HD + HALF : HD + HALF + 1] * mine_gain + seen[:, HD + HALF : HD + HALF + 1] * seen_gain
    mine_gain, seen_gain = mine_gain / total, seen_gain / total
    head_out = mine[:, :HD] * mine_gain + seen[:, :HD] * seen_gain
    delta = jnp.sum(grad.astype(F32) * head_out, axis=1, keepdims=True)
    probs = probs_ref[...] * mine_gain
    stores = []
    for kind in (1, 0):
        there = slice(kind * HD, (kind + 1) * HD)
        if kind == 1:
            total = dot(probs.astype(BF16), grad, (0, 0))
        else:
            score_grad = (probs * (dot(grad, values, (1, 1)) - delta)).astype(BF16)
            total = dot(score_grad, query, (0, 0)) * SCALE
        total = total.astype(BF16).reshape(SPLIT, 2, 8, 4 // SPLIT, 16, HD)
        for part in range(SPLIT):
            for zh in range(2):
                rows = slice(zh * 16, (zh + 1) * 16)
                staged[:, share_of(part), :, rows, there] = total[part, zh]
        store = pltpu.make_async_copy(
            staged.at[:, :, :, :, there], kv_grad_ref.at[:, :, :, :, there], sems.at[kind]
        )
        store.start()
        stores.append(store)
    query_grad = dot(score_grad, keys, (1, 0)) * SCALE
    own_ref[...] = query_grad[:ROWS]
    send_ref[...] = query_grad[ROWS:]
    wait_all(stores)


def sum_kernel(parts_ref, out_ref):
    total = parts_ref[0].astype(F32)
    for b in range(1, 8):
        total = total + parts_ref[b].astype(F32)
    low = total.astype(BF16)
    row, source = iota((256, 128), 0), iota((256, 128), 1)
    place = row // 4 % 4 * 32 + row // 16 * 2 + row % 2
    pick_key = ((place == source) & (row // 2 % 2 == 0)).astype(BF16)
    pick_value = ((place == source) & (row // 2 % 2 == 1)).astype(BF16)
    out_ref[...] = (dot(pick_key, low[:, :HD], (1, 0)) + dot(pick_value, low[:, HD:], (1, 0))).astype(BF16)


def last_kernel(parts_ref, key_ref, value_ref):
    parts = parts_ref[...].astype(F32)
    both = parts[:128] + parts[128:]
    total = [sum(both[16 * g + 4 * xl : 16 * g + 4 * xl + 4] for xl in range(4)) for g in range(8)]
    key_ref[...] = jnp.concatenate([one[:2] for one in total], axis=1).astype(BF16)
    value_ref[...] = jnp.concatenate([one[2:] for one in total], axis=1).astype(BF16)


def swap(array):
    return lax.ppermute(array, "core", [(0, 1), (1, 0)])


def exchange(array, axes):
    return lax.all_to_all(array, axes, split_axis=0, concat_axis=0, tiled=True)


def body(out_grad, expert_rows, expert_index, combine, head_query, head_key, head_value, out_weight):
    (packed,) = call(
        pack_kernel,
        [((N_CTX, PACK, HD), BF16)],
        expert_rows.reshape(N_CTX, CAP, HD),
        head_key,
        head_value,
        far=(0, 1, 2),
        far_outs=(0,),
        scratch=[
            pltpu.VMEM((ROWS, HD), BF16),
            pltpu.VMEM((ROWS, HD), BF16),
            pltpu.VMEM((N_CTX, PACK, HD), BF16),
            pltpu.SemaphoreType.DMA((4,)),
        ],
    )
    received = exchange(packed, CTX)
    own_weight, send_weight, token = call(
        weight_kernel,
        [(WEIGHTS, BF16)] * 2 + [((8, HD), F32)],
        out_weight,
        far=(0,),
        far_outs=(0, 1),
        scratch=[
            pltpu.VMEM((ROWS, 2 * N_PEERS * HD), BF16),
            pltpu.VMEM(WEIGHTS, BF16),
            pltpu.VMEM(WEIGHTS, BF16),
            pltpu.SemaphoreType.DMA((CHUNKS + 2,)),
        ],
    )
    mate_weight = swap(send_weight)
    mate_query = swap(head_query)
    (onehot,) = call(slots_kernel, [((2 * ROWS, EXPERTS * CAP), BF16)], expert_index)
    residual_grad, residual_send = call(
        residual_kernel,
        [((ROWS, HD), BF16), ((N_PEERS, ROWS, HD), BF16)],
        out_grad,
        received,
        onehot,
        combine,
        token,
        free=(4,),
        far_outs=(1,),
        scratch=[pltpu.VMEM((N_PEERS, ROWS, HD), BF16), pltpu.SemaphoreType.DMA((4,))],
    )
    held = received[:, CAP:]
    near = [lax.ppermute(held, "y", [(n, n ^ p) for n in range(8)]) for p in range(1, SPLIT)]
    blocks = exchange(residual_send, PEERS)
    probs, stat = call(
        forward_kernel,
        [((2 * ROWS, KEYS), F32), ((2 * ROWS, 2 * HD), F32)],
        head_query,
        mate_query,
        received,
        *near,
    )
    seen = swap(stat)
    (part,) = call(
        project_kernel,
        [((ROWS, 2 * HD), F32)],
        blocks,
        own_weight,
        mate_weight,
        far=(1, 2),
        scratch=[
            pltpu.VMEM(WEIGHTS, BF16),
            pltpu.VMEM(WEIGHTS, BF16),
            pltpu.SemaphoreType.DMA((2, CHUNKS)),
        ],
    )
    other = swap(part)
    kv_grad, own_grad, send_grad = call(
        backward_kernel,
        [((8, SPLIT, 4 // SPLIT, 32, 2 * HD), BF16), ((ROWS, HD), F32), ((ROWS, HD), F32)],
        part,
        other,
        head_query,
        mate_query,
        probs,
        stat,
        seen,
        received,
        *near,
        far_outs=(0,),
        scratch=[
            pltpu.VMEM((8, SPLIT, 4 // SPLIT, 32, 2 * HD), BF16),
            pltpu.SemaphoreType.DMA((2,)),
        ],
    )
    kv_parts = exchange(kv_grad.reshape(8, 128, 2 * HD), ("y",))
    query_grad = (own_grad + swap(send_grad)).astype(BF16)
    (kv_sum,) = call(sum_kernel, [((256, HD), BF16)], kv_parts)
    final = exchange(kv_sum.reshape(64, 4, HD), ("zh", "zl", "xh", "xl"))
    key_grad, value_grad = call(
        last_kernel, [((2, 8 * HD), BF16), ((2, 8 * HD), BF16)], final.reshape(256, HD)
    )
    return residual_grad, query_grad, key_grad, value_grad


def solution(mesh):
    fine = Mesh(mesh.devices.reshape(SIZES), AXES)
    in_specs = (
        P(CTX, EXP),
        P(CTX, None, EXP),
        P(CTX, None),
        P(CTX, None),
        P(CTX, EXP),
        P(CTX, None),
        P(CTX, None),
        P(EXP, None),
    )
    out_specs = (P(CTX, EXP), P(CTX, EXP), P(CTX + EXP, None), P(CTX + EXP, None))
    return jax.shard_map(body, mesh=fine, in_specs=in_specs, out_specs=out_specs, check_vma=False)
```

```python
import math

import jax
import jax.numpy as jnp
from jax import lax
from jax.experimental import pallas as pl
from jax.experimental.pallas import tpu as pltpu
from jax.sharding import Mesh
from jax.sharding import PartitionSpec as P

HD = 128
SCALE = 1.0 / math.sqrt(HD)
LOW = -1e30
AXES = ("zh", "y", "zl", "xh", "xl", "core")
SIZES = (2, 8, 4, 2, 4, 2)
CTX = ("zh", "y")
EXP = ("zl", "xh", "xl", "core")
PEERS = ("zl", "xh", "xl")
N_CTX = 16
ROWS = 128
EXPERTS = 16
CAP = 32
N_PEERS = 32
HALF = 64
KEYS = N_CTX * HALF
SPLIT = 4
SHARE = HALF // SPLIT
PACK = CAP + 2 * SHARE
F32 = jnp.float32
BF16 = jnp.bfloat16
VMEM = pl.BlockSpec(memory_space=pltpu.VMEM)
HBM = pl.BlockSpec(memory_space=pltpu.HBM)
PARAMS = pltpu.CompilerParams(vmem_limit_bytes=16 * 1024 * 1024)


def in_hbm(array):
    return pltpu.with_memory_space_constraint(array, pltpu.HBM)


def call(kernel, outs, *operands, far=(), free=(), far_outs=(), scratch=()):
    spaces = {n: HBM for n in far} | {n: pl.BlockSpec(memory_space=pl.ANY) for n in free}
    return pl.pallas_call(
        kernel,
        out_shape=[
            pltpu.HBM(shape, kind) if n in far_outs else jax.ShapeDtypeStruct(shape, kind)
            for n, (shape, kind) in enumerate(outs)
        ],
        in_specs=[spaces.get(n, VMEM) for n in range(len(operands))],
        out_specs=[HBM if n in far_outs else VMEM for n in range(len(outs))],
        scratch_shapes=scratch,
        compiler_params=PARAMS,
    )(*[in_hbm(operand) if n in far else operand for n, operand in enumerate(operands)])


def dot(a, b, dims):
    return lax.dot_general(a, b, ((dims[:1], dims[1:]), ((), ())), preferred_element_type=F32)


def iota(shape, dim):
    return lax.broadcasted_iota(jnp.int32, shape, dim)


def key_row(number):
    xl, zl, xh, i = number // 16, (number // 4) % 4, (number // 2) % 2, number % 2
    return zl * 32 + xh * 16 + xl * 4 + lax.axis_index("core") * 2 + i


def position(block, row):
    return jnp.where(row < 64, block, 2 * N_CTX - 1 - block) * 64 + row % 64


def share_of(part):
    return lax.bitwise_xor(lax.axis_index("y") % SPLIT, part)


def joined_kv(pack_ref, *near_refs):
    return [
        jnp.concatenate(
            [pack_ref[:, CAP + at : CAP + at + SHARE].reshape(N_CTX * SHARE, HD)]
            + [near_ref[:, at : at + SHARE].reshape(N_CTX * SHARE, HD) for near_ref in near_refs],
            axis=0,
        )
        for at in (0, SHARE)
    ]


def start_all(copies):
    for copy in copies:
        copy.start()


def wait_all(copies):
    for copy in copies:
        copy.wait()


def pack_kernel(rows_ref, key_ref, value_ref, out_ref, key_own, value_own, packed, sems):
    group = lax.axis_index("zl") * 2 + lax.axis_index("xh")
    columns = pl.ds(pl.multiple_of(group * HD, HD), HD)
    rows = pltpu.make_async_copy(rows_ref, packed.at[:, :CAP], sems.at[2])
    loads = [
        pltpu.make_async_copy(key_ref.at[:, columns], key_own, sems.at[0]),
        pltpu.make_async_copy(value_ref.at[:, columns], value_own, sems.at[1]),
    ]
    start_all(loads + [rows])
    select = (iota((HALF, ROWS), 1) == key_row(iota((HALF, ROWS), 0))).astype(BF16)
    wait_all(loads)
    keys = dot(select, key_own[...], (1, 0)).astype(BF16)
    values = dot(select, value_own[...], (1, 0)).astype(BF16)
    for c in range(N_CTX):
        there = slice(c % SPLIT * SHARE, (c % SPLIT + 1) * SHARE)
        packed[c, CAP : CAP + SHARE] = keys[there]
        packed[c, CAP + SHARE :] = values[there]
    rows.wait()
    store = pltpu.make_async_copy(packed, out_ref, sems.at[3])
    store.start()
    store.wait()


def weight_kernel(weight_ref, own_ref, send_ref, token_ref, whole, own, send, sems):
    core = lax.axis_index("core")
    span = 8
    loads = [
        pltpu.make_async_copy(
            weight_ref.at[:, 2 * a * HD : 2 * (a + span) * HD],
            whole.at[:, 2 * a * HD : 2 * (a + span) * HD],
            sems.at[a // span],
        )
        for a in range(0, N_PEERS, span)
    ]
    start_all(loads)
    for a in range(0, N_PEERS, span):
        loads[a // span].wait()
        for b in range(a, a + span):
            within = slice((b - a) * HD, (b - a + 1) * HD)
            own_at = pl.ds(pl.multiple_of((2 * b + core) * HD, HD), HD)
            send_at = pl.ds(pl.multiple_of((2 * b + 1 - core) * HD, HD), HD)
            own[a // span, :, within] = whole[:, own_at]
            send[:, b * HD : (b + 1) * HD] = whole[:, send_at]
    stores = [
        pltpu.make_async_copy(own, own_ref, sems.at[4]),
        pltpu.make_async_copy(send, send_ref, sems.at[5]),
    ]
    start_all(stores)
    token_ref[...] = jnp.zeros_like(token_ref)
    wait_all(stores)


def slots_kernel(index_ref, out_ref):
    index = index_ref[...]
    experts = iota((ROWS, HD), 1)
    named = [index[:, k : k + 1] == experts for k in range(2)]
    both = (named[0] | named[1]).astype(BF16)
    before = (iota((ROWS, ROWS), 1) < iota((ROWS, ROWS), 0)).astype(BF16)
    earlier = dot(before, both, (1, 0))
    for k in range(2):
        slot = jnp.sum(jnp.where(named[k], earlier, 0.0), axis=1, keepdims=True).astype(jnp.int32)
        place = index[:, k : k + 1] * CAP + slot
        wide = iota((ROWS, EXPERTS * CAP), 1) == place
        out_ref[k * ROWS : (k + 1) * ROWS] = wide.astype(BF16)


def residual_kernel(
    grad_ref, pack_ref, onehot_ref, combine_ref, _token, out_ref, send_ref, copied, sems
):
    rows = pack_ref[:, :CAP].reshape(EXPERTS * CAP, HD)
    picked = dot(onehot_ref[...], rows, (1, 0))
    combine = combine_ref[...]
    moe = combine[:, 0:1] * picked[:ROWS] + combine[:, 1:2] * picked[ROWS:]
    residual = (grad_ref[...].astype(F32) + moe).astype(BF16)
    span = 8
    copies = []
    for a in range(0, N_PEERS, span):
        for b in range(a, a + span):
            copied[b] = residual
        copy = pltpu.make_async_copy(
            copied.at[a : a + span], send_ref.at[a : a + span], sems.at[a // span]
        )
        copy.start()
        copies.append(copy)
    out_ref[...] = residual
    wait_all(copies)


def forward_kernel(query_ref, mate_ref, pack_ref, *refs):
    *near_refs, probs_ref, stat_ref, staged, sem = refs
    block = lax.axis_index("zh") * 8 + lax.axis_index("y")
    query = jnp.concatenate([query_ref[...], mate_ref[...]], axis=0)
    keys, values = joined_kv(pack_ref, *near_refs)
    row = iota((2 * ROWS, 1), 0) % ROWS
    number = iota((1, KEYS), 1)
    source = number % (KEYS // SPLIT) // SHARE
    held = share_of(number // (KEYS // SPLIT)) * SHARE + number % SHARE
    allowed = position(source, key_row(held)) <= position(block, row)
    scores = jnp.where(allowed, dot(query, keys, (1, 1)) * SCALE, LOW)
    top = jnp.max(scores, axis=1, keepdims=True)
    probs = jnp.where(allowed, jnp.exp(scores - top), 0.0)
    total = jnp.sum(probs, axis=1, keepdims=True)
    staged[...] = probs
    store = pltpu.make_async_copy(staged, probs_ref, sem.at[0])
    store.start()
    stat_ref[:, :HD] = dot(probs.astype(BF16), values, (1, 0))
    stat_ref[:, HD:] = jnp.where(iota((2 * ROWS, HD), 1) < HALF, top, total)
    store.wait()


def project_kernel(blocks_ref, own_ref, mate_ref, out_ref, own, sems):
    span = 8
    copies = [
        pltpu.make_async_copy(own_ref.at[a // span], own.at[a // span], sems.at[a // span])
        for a in range(0, N_PEERS, span)
    ]
    start_all(copies)
    total = [jnp.zeros((ROWS, HD), F32)] * 2
    parts = []
    for a in range(0, N_PEERS, span):
        part = jnp.concatenate([blocks_ref[b] for b in range(a, a + span)], axis=1)
        parts.append(part)
        total[1] = total[1] + dot(part, mate_ref[:, a * HD : (a + span) * HD], (1, 1))
    for k, part in enumerate(parts):
        copies[k].wait()
        total[0] = total[0] + dot(part, own[k], (1, 1))
    out_ref[:, :HD] = total[0]
    out_ref[:, HD:] = total[1]


def backward_kernel(
    part_ref, other_ref, query_ref, mate_ref, probs_ref, stat_ref, seen_ref, pack_ref, *refs
):
    *near_refs, kv_grad_ref, own_ref, send_ref = refs
    grad = jnp.concatenate(
        [
            part_ref[:, :HD] + other_ref[:, HD:],
            part_ref[:, HD:] + other_ref[:, :HD],
        ],
        axis=0,
    ).astype(BF16)
    query = jnp.concatenate([query_ref[...], mate_ref[...]], axis=0)
    keys, values = joined_kv(pack_ref, *near_refs)
    mine = stat_ref[...]
    seen = jnp.concatenate([seen_ref[ROWS:], seen_ref[:ROWS]], axis=0)
    top_mine, top_seen = mine[:, HD : HD + 1], seen[:, HD : HD + 1]
    top = jnp.maximum(top_mine, top_seen)
    mine_gain, seen_gain = jnp.exp(top_mine - top), jnp.exp(top_seen - top)
    total = mine[:, HD + HALF : HD + HALF + 1] * mine_gain + seen[:, HD + HALF : HD + HALF + 1] * seen_gain
    mine_gain, seen_gain = mine_gain / total, seen_gain / total
    head_out = mine[:, :HD] * mine_gain + seen[:, :HD] * seen_gain
    delta = jnp.sum(grad.astype(F32) * head_out, axis=1, keepdims=True)
    probs = probs_ref[...] * mine_gain
    score_grad = (probs * (dot(grad, values, (1, 1)) - delta)).astype(BF16)
    shape = (SPLIT, 2, 8, 4 // SPLIT, 16, HD)
    key_grad = (dot(score_grad, query, (0, 0)) * SCALE).astype(BF16).reshape(shape)
    value_grad = dot(probs.astype(BF16), grad, (0, 0)).astype(BF16).reshape(shape)
    for part in range(SPLIT):
        share = share_of(part)
        for zh in range(2):
            there = slice(zh * 16, (zh + 1) * 16)
            kv_grad_ref[:, share, :, there, :HD] = key_grad[part, zh]
            kv_grad_ref[:, share, :, there, HD:] = value_grad[part, zh]
    query_grad = dot(score_grad, keys, (1, 0)) * SCALE
    own_ref[...] = query_grad[:ROWS]
    send_ref[...] = query_grad[ROWS:]


def sum_kernel(parts_ref, out_ref):
    total = parts_ref[0].astype(F32)
    for b in range(1, 32):
        total = total + parts_ref[b].astype(F32)
    low = total.astype(BF16)
    row, source = iota((64, 32), 0), iota((64, 32), 1)
    place = row // 4 * 2 + row % 2
    pick_key = ((place == source) & (row // 2 % 2 == 0)).astype(BF16)
    pick_value = ((place == source) & (row // 2 % 2 == 1)).astype(BF16)
    out_ref[...] = (dot(pick_key, low[:, :HD], (1, 0)) + dot(pick_value, low[:, HD:], (1, 0))).astype(BF16)


def last_kernel(parts_ref, key_ref, value_ref):
    parts = parts_ref[...].astype(F32)
    total = parts[:32] + parts[32:]
    key_ref[...] = jnp.concatenate([total[4 * g : 4 * g + 2] for g in range(8)], axis=1).astype(BF16)
    value_ref[...] = jnp.concatenate([total[4 * g + 2 : 4 * g + 4] for g in range(8)], axis=1).astype(BF16)


def swap(array):
    return lax.ppermute(array, "core", [(0, 1), (1, 0)])


def exchange(array, axes):
    return lax.all_to_all(array, axes, split_axis=0, concat_axis=0, tiled=True)


def body(out_grad, expert_rows, expert_index, combine, head_query, head_key, head_value, out_weight):
    (packed,) = call(
        pack_kernel,
        [((N_CTX, PACK, HD), BF16)],
        expert_rows.reshape(N_CTX, CAP, HD),
        head_key,
        head_value,
        far=(0, 1, 2),
        far_outs=(0,),
        scratch=[
            pltpu.VMEM((ROWS, HD), BF16),
            pltpu.VMEM((ROWS, HD), BF16),
            pltpu.VMEM((N_CTX, PACK, HD), BF16),
            pltpu.SemaphoreType.DMA((4,)),
        ],
    )
    received = exchange(packed, CTX)
    own_weight, send_weight, token = call(
        weight_kernel,
        [((4, ROWS, 8 * HD), BF16), ((ROWS, N_PEERS * HD), BF16), ((8, HD), F32)],
        out_weight,
        far=(0,),
        far_outs=(0, 1),
        scratch=[
            pltpu.VMEM((ROWS, 2 * N_PEERS * HD), BF16),
            pltpu.VMEM((4, ROWS, 8 * HD), BF16),
            pltpu.VMEM((ROWS, N_PEERS * HD), BF16),
            pltpu.SemaphoreType.DMA((6,)),
        ],
    )
    mate_weight = swap(send_weight)
    mate_query = swap(head_query)
    (onehot,) = call(slots_kernel, [((2 * ROWS, EXPERTS * CAP), BF16)], expert_index)
    residual_grad, residual_send = call(
        residual_kernel,
        [((ROWS, HD), BF16), ((N_PEERS, ROWS, HD), BF16)],
        out_grad,
        received,
        onehot,
        combine,
        token,
        free=(4,),
        far_outs=(1,),
        scratch=[pltpu.VMEM((N_PEERS, ROWS, HD), BF16), pltpu.SemaphoreType.DMA((4,))],
    )
    held = received[:, CAP:]
    near = [lax.ppermute(held, "y", [(n, n ^ p) for n in range(8)]) for p in range(1, SPLIT)]
    blocks = exchange(residual_send, PEERS)
    probs, stat = call(
        forward_kernel,
        [((2 * ROWS, KEYS), F32), ((2 * ROWS, 2 * HD), F32)],
        head_query,
        mate_query,
        received,
        *near,
        far_outs=(0,),
        scratch=[pltpu.VMEM((2 * ROWS, KEYS), F32), pltpu.SemaphoreType.DMA((1,))],
    )
    seen = swap(stat)
    (part,) = call(
        project_kernel,
        [((ROWS, 2 * HD), F32)],
        blocks,
        own_weight,
        mate_weight,
        far=(1,),
        scratch=[pltpu.VMEM((4, ROWS, 8 * HD), BF16), pltpu.SemaphoreType.DMA((4,))],
    )
    other = swap(part)
    kv_grad, own_grad, send_grad = call(
        backward_kernel,
        [((8, SPLIT, 4 // SPLIT, 32, 2 * HD), BF16), ((ROWS, HD), F32), ((ROWS, HD), F32)],
        part,
        other,
        head_query,
        mate_query,
        probs,
        stat,
        seen,
        received,
        *near,
    )
    kv_parts = exchange(kv_grad.reshape(32, 32, 2 * HD), ("y", "xl"))
    query_grad = (own_grad + swap(send_grad)).astype(BF16)
    (kv_sum,) = call(sum_kernel, [((64, HD), BF16)], kv_parts)
    final = exchange(kv_sum.reshape(16, 4, HD), ("zh", "zl", "xh"))
    key_grad, value_grad = call(
        last_kernel, [((2, 8 * HD), BF16), ((2, 8 * HD), BF16)], final.reshape(64, HD)
    )
    return residual_grad, query_grad, key_grad, value_grad


def solution(mesh):
    fine = Mesh(mesh.devices.reshape(SIZES), AXES)
    in_specs = (
        P(CTX, EXP),
        P(CTX, None, EXP),
        P(CTX, None),
        P(CTX, None),
        P(CTX, EXP),
        P(CTX, None),
        P(CTX, None),
        P(EXP, None),
    )
    out_specs = (P(CTX, EXP), P(CTX, EXP), P(CTX + EXP, None), P(CTX + EXP, None))
    return jax.shard_map(body, mesh=fine, in_specs=in_specs, out_specs=out_specs, check_vma=False)
```
